512 devices in a mesh: fsdp: 64 (over z, y), expert: 8 (over x, core).
Axes of the slice: x: 4, y: 4, z: 16, core: 2. Of those that a mesh axis runs over, the one named last changes fastest.
Arguments:
- grad: float32 [16, 3, 3584, 1024], P('expert', None, 'fsdp'), may hold values from -1000 to 1000
- momentum: float32 [16, 3, 3584, 1024], P('expert', None, 'fsdp'), may hold values from -120 to 120
- owners: int32 [16, 3], replicated, may hold values from 0 to 63, as said below
Outputs:
- momentum_new: float32 [16, 3, 3584, 1024], P('expert', None, 'fsdp')
- update: bfloat16 [16, 3, 3584, 1024], P('expert', None, 'fsdp')
- owned_rms: float32 [64], P('fsdp')
The draws below stay inside these ranges and needn't reach their ends.
Inputs may be any that keep to these rules, and one draw needn't show every extreme that they name: `owners`: all 48 entries are different.
All inputs are finite; a program needn't handle non-finite values.
Results may differ from the reference program's by a relative error of at most 0.009.
Values may be sent and summed in bfloat16 or wider, within the bound.
No kernel may reach another device: no remote copies, remote signals or barrier semaphores. Data moves between devices by JAX's collectives and lax.ppermute only.
A program may use at most 64 MiB of HBM per device.

```python
import math
import jax
import jax.numpy as jnp
from jax import lax

D = 3584
FF = 1024
ITERS = 2
EXPERTS = 16
N_FSDP = 64
N_EXPERT = 8


def draw_grad(key, part):
    key = jax.random.fold_in(key, 11)
    key_base, key_rows, key_cols = jax.random.split(key, 3)
    shape = (EXPERTS, 3, D, FF)
    rows = jnp.exp(jax.random.uniform(key_rows, (EXPERTS, 3, D, 1), jnp.float32) * math.log(10.0))
    cols = jnp.exp(jax.random.uniform(key_cols, (EXPERTS, 3, 1, FF), jnp.float32) * math.log(10.0))
    values = jnp.clip(jax.random.normal(key_base, shape, jnp.float32), -5.0, 5.0) * rows * cols
    return values.astype(jnp.float32)


def draw_owners(key, part):
    key = jax.random.fold_in(key, 23)
    order = jax.random.permutation(key, N_FSDP)
    return order[:EXPERTS * 3].reshape(EXPERTS, 3).astype(jnp.int32)


def block_scale(own_key, shape, pieces, least, top_value):
    gain, own = 1.0, jax.random.fold_in(own_key, 6)
    for dim, parts in pieces:
        draws = jnp.exp(jax.random.uniform(jax.random.fold_in(own, dim), (parts,), jnp.float32, least / len(pieces), top_value / len(pieces)))
        gain = gain * jnp.repeat(draws, shape[dim] // parts).reshape([-1 if axis == dim else 1 for axis in range(len(shape))])
    return gain


def noise(own_key, extent, scale, bound, shards=(), kind=jnp.bfloat16):
    entries = jax.random.normal(own_key, extent, jnp.float32) * scale
    if len(shards) > 0:
        entries = block_scale(own_key, extent, shards, -0.22, 0.18) * entries
    return jnp.clip(entries, min=-bound, max=bound).astype(kind)


def setup_inputs(seed: int = 0) -> dict:
    seeds = jax.random.split(jax.random.key(seed), 4)
    grad = draw_grad(jax.random.fold_in(seeds[3], 71), 0)
    momentum = noise(seeds[1], (EXPERTS, 3, D, FF), 20.0, 120.0, ((0, 8), (2, 64)), jnp.float32)
    owners = draw_owners(jax.random.fold_in(seeds[3], 71), 0)
    return dict(grad=grad, momentum=momentum, owners=owners)


MU = 0.95
COEF_P = 3.4445
COEF_Q = -4.775
COEF_T = 2.0315

def newton_schulz(matrix):
    current = matrix
    norm_sq = jnp.float32(0.0)
    subrows = D // (N_FSDP * N_EXPERT)
    for step in range(ITERS):
        blocks = current.reshape(N_FSDP, N_EXPERT, subrows, FF).astype(jnp.float32)
        partial_value = jnp.einsum('fjtc,fjtd->jcd', blocks, blocks, precision=lax.Precision.HIGHEST)
        rounded = lax.optimization_barrier(partial_value.astype(jnp.bfloat16))
        gram = lax.optimization_barrier(jnp.sum(rounded.astype(jnp.float32), axis=0))
        gram_half = gram.astype(jnp.bfloat16)
        if step == 0:
            norm_sq = jnp.trace(gram)
            scale = lax.rsqrt(norm_sq)
            coef_p = COEF_P * scale
            coef_q = COEF_Q * scale * scale * scale
            coef_t = COEF_T * scale * scale * scale * scale * scale
        else:
            coef_p = jnp.float32(COEF_P)
            coef_q = jnp.float32(COEF_Q)
            coef_t = jnp.float32(COEF_T)
        if step == ITERS - 1:
            factor = jnp.float32(math.sqrt(D))
            coef_p = coef_p * factor
            coef_q = coef_q * factor
            coef_t = coef_t * factor
        product = jnp.dot(current, gram_half, preferred_element_type=jnp.float32)
        second = jnp.dot(product.astype(jnp.bfloat16), gram_half, preferred_element_type=jnp.float32)
        current = (coef_p * current.astype(jnp.float32) + coef_q * product + coef_t * second).astype(jnp.bfloat16)
    return (current, norm_sq)

def reference(grad, momentum, owners):
    momentum_new = MU * momentum + grad
    blended = (grad + MU * momentum_new).astype(jnp.bfloat16)
    flat = blended.reshape(EXPERTS * 3, D, FF)
    finals, norms = lax.map(newton_schulz, flat)
    update = finals.reshape(EXPERTS, 3, D, FF)
    rms_values = jnp.sqrt(norms / (D * FF))
    owned_rms = jnp.zeros((N_FSDP,), jnp.float32).at[owners.reshape(-1).astype(jnp.int32)].set(rms_values)
    return (momentum_new, update, owned_rms)
```

```python
import math

import jax
import jax.numpy as jnp
from jax import lax
from jax.experimental import pallas as pl
from jax.experimental.pallas import tpu as pltpu
from jax.sharding import Mesh
from jax.sharding import PartitionSpec as P

D = 3584
FF = 1024
HALF = FF // 2
BLK = 256
SHARD = 56
ROWS = 64
CHUNK = 272
EXTRA = 16

MU = 0.95
COEF_P = 3.4445
COEF_Q = -4.775
COEF_T = 2.0315


F32 = jnp.float32
BF16 = jnp.bfloat16
VMEM = pl.BlockSpec(memory_space=pltpu.VMEM)
SMEM = pl.BlockSpec(memory_space=pltpu.SMEM)


def params(mib):
    return pltpu.CompilerParams(vmem_limit_bytes=mib * 1024 * 1024)


def dot(a, b):
    return jnp.dot(a, b, preferred_element_type=F32)


def dot_rows(a, b):
    return lax.dot_general(a, b, (((0,), (0,)), ((), ())), preferred_element_type=F32)


def blend_kernel(c_ref, grad_ref, mom_ref, new_ref, keep_ref, send_ref):
    first = c_ref[0] == 0
    grad = grad_ref[0]
    new = MU * mom_ref[0] + grad
    new_ref[0] = new
    blended = (grad + MU * new).astype(BF16)
    left, right = blended[:, :HALF], blended[:, HALF:]
    keep_ref[0] = jnp.where(first, left, right)
    send_ref[0] = jnp.where(first, right, left)


def blend(core, grad, momentum):
    count = grad.shape[0]
    full = pl.BlockSpec((1, SHARD, FF), lambda i: (i, 0, 0))
    half = pl.BlockSpec((1, SHARD, HALF), lambda i: (i, 0, 0))
    return pl.pallas_call(
        blend_kernel,
        grid=(count,),
        in_specs=[SMEM, full, full],
        out_specs=[full, half, half],
        out_shape=[
            jax.ShapeDtypeStruct((count, SHARD, FF), F32),
            jax.ShapeDtypeStruct((count, SHARD, HALF), BF16),
            jax.ShapeDtypeStruct((count, SHARD, HALF), BF16),
        ],
        compiler_params=params(16),
    )(core, grad, momentum)


def pack_kernel(c_ref, keep_ref, recv_ref, out_ref):
    c = c_ref[0]
    pad = jnp.zeros((ROWS - SHARD, HALF), F32)
    for k in range(4):
        for q in range(4):
            if k == 3:
                out_ref[k * 4 + q] = jnp.zeros((ROWS, HALF), BF16)
                continue
            i = (q % 2) * 3 + k
            piece = jnp.where(c == q // 2, keep_ref[i], recv_ref[i]).astype(F32)
            out_ref[k * 4 + q] = jnp.concatenate([piece, pad], axis=0).astype(BF16)


def pack(core, keep, recv):
    return pl.pallas_call(
        pack_kernel,
        in_specs=[SMEM, VMEM, VMEM],
        out_specs=VMEM,
        out_shape=jax.ShapeDtypeStruct((16, ROWS, HALF), BF16),
        compiler_params=params(16),
    )(core, keep, recv)


def index_grid(shape):
    return lax.broadcasted_iota(jnp.int32, shape, 0), lax.broadcasted_iota(jnp.int32, shape, 1)


def gram_kernel(c_ref, own_ref, oth_ref, out_ref, trace_ref):
    first = c_ref[0] == 0
    row, col = index_grid((BLK, BLK))
    x0, x1 = own_ref[:, :BLK], own_ref[:, BLK:]
    y0, y1 = oth_ref[:, :BLK], oth_ref[:, BLK:]
    g00, g11 = dot_rows(x0, x0), dot_rows(x1, x1)
    diag0 = jnp.sum(jnp.where(row == col, g00, 0.0), axis=0, keepdims=True)
    diag1 = jnp.sum(jnp.where(row == col, g11, 0.0), axis=0, keepdims=True)
    out_ref[0:BLK] = jnp.where(row <= col, g00, g11).astype(BF16)
    out_ref[BLK : 2 * BLK] = dot_rows(x0, x1).astype(BF16)
    out_ref[2 * BLK : 3 * BLK] = dot_rows(x0, jnp.where(first, y0, y1)).astype(BF16)
    out_ref[3 * BLK : 4 * BLK] = dot_rows(x1, jnp.where(first, y1, y0)).astype(BF16)
    out_ref[4 * BLK :] = jnp.broadcast_to(diag1, (4 * CHUNK - 4 * BLK, BLK)).astype(BF16)
    total = jnp.sum(diag0 + diag1, axis=1, keepdims=True)
    trace_ref[...] = jnp.broadcast_to(total, trace_ref.shape)


def partial_gram(core, own, oth):
    return pl.pallas_call(
        gram_kernel,
        in_specs=[SMEM, VMEM, VMEM],
        out_specs=[VMEM, VMEM],
        out_shape=[
            jax.ShapeDtypeStruct((4 * CHUNK, BLK), BF16),
            jax.ShapeDtypeStruct((16, 128), F32),
        ],
        compiler_params=params(32),
    )(core, own, oth)


def sum_kernel(parts_ref, t0_ref, t1_ref, t2_ref, t3_ref, out_ref):
    total = parts_ref[0].astype(F32) + parts_ref[1].astype(F32)
    total = total + (parts_ref[2].astype(F32) + parts_ref[3].astype(F32))
    out_ref[:CHUNK] = total.astype(BF16)
    row, _ = index_grid((EXTRA, 128))
    value = jnp.where(row < 4, t0_ref[...], t1_ref[...])
    value = jnp.where(row < 8, value, jnp.where(row < 12, t2_ref[...], t3_ref[...]))
    high = value.astype(BF16)
    out_ref[CHUNK:, :128] = high
    out_ref[CHUNK:, 128:] = (value - high.astype(F32)).astype(BF16)


def sum_parts(parts, traces):
    return pl.pallas_call(
        sum_kernel,
        in_specs=[VMEM] * 5,
        out_specs=VMEM,
        out_shape=jax.ShapeDtypeStruct((CHUNK + EXTRA, BLK), BF16),
        compiler_params=params(16),
    )(parts, *traces)


def unpack(ref):
    blocks, at = [], 0
    for _ in range(4):
        pieces, need = [], BLK
        while need:
            chunk, offset = divmod(at, CHUNK)
            take = min(need, CHUNK - offset)
            pieces.append(ref[chunk, offset : offset + take])
            at, need = at + take, need - take
        piece = pieces[0] if len(pieces) == 1 else jnp.concatenate(pieces, axis=0)
        blocks.append(piece.astype(F32))
    offset = at - 3 * CHUNK
    return blocks, ref[3, offset : offset + 16].astype(F32)[0:1]


def polynomial_kernel(
    c_ref, own_ref, oth_ref, xo_ref, xt_ref, out_ref, a32, ab, m32, mb, c32, cb, gb, w32, nb, wb
):
    first = c_ref[0] == 0
    row, col = index_grid((BLK, BLK))
    (d_o, o01, p2, p3), e_o = unpack(own_ref)
    (d_t, t01, r2, r3), e_t = unpack(oth_ref)

    extra = own_ref[0, CHUNK:].astype(F32) + oth_ref[0, CHUNK:].astype(F32)
    for i in range(1, 4):
        extra = extra + (own_ref[i, CHUNK:].astype(F32) + oth_ref[i, CHUNK:].astype(F32))
    norms = extra[:, :128] + extra[:, 128:]
    scale = lax.rsqrt(norms[0:1, 0:1])
    square = scale * scale

    def put(i, j, value):
        value = value * square
        a32[i * BLK : (i + 1) * BLK, j * BLK : (j + 1) * BLK] = value
        ab[i * BLK : (i + 1) * BLK, j * BLK : (j + 1) * BLK] = value.astype(BF16)

    def put_pair(i, j, value, turned):
        put(i, j, value)
        put(j, i, turned)

    for base, packed, edge, off in ((0, d_o, e_o, o01), (2, d_t, e_t, t01)):
        turned = packed.T
        put(base, base, jnp.where(row <= col, packed, turned))
        upper = jnp.where(row == col, jnp.broadcast_to(edge, (BLK, BLK)), turned)
        put(base + 1, base + 1, jnp.where(row > col, packed, upper))
        put_pair(base, base + 1, off, off.T)
    p2t, p3t, r2t, r3t = p2.T, p3.T, r2.T, r3.T
    put_pair(0, 2, jnp.where(first, p2, r2t), jnp.where(first, p2t, r2))
    put_pair(0, 3, jnp.where(first, r3t, p2), jnp.where(first, r3, p2t))
    put_pair(1, 2, jnp.where(first, r2t, p3), jnp.where(first, r2, p3t))
    put_pair(1, 3, jnp.where(first, p3, r3t), jnp.where(first, p3t, r3))

    blocks = [slice(i * BLK, (i + 1) * BLK) for i in range(4)]
    for s in blocks:
        poly = COEF_Q * a32[s] + COEF_T * dot(ab[s], ab[...])
        m32[s] = poly[:, :HALF]
        mb[s] = poly.astype(BF16)
    for s in blocks:
        prod = COEF_P * a32[s] + dot(ab[s], mb[...])
        c32[s] = prod
        cb[s] = prod.astype(BF16)
    for s in blocks:
        gram = COEF_P * c32[s] + dot(cb[s], mb[...])
        c32[s] = gram
        gb[s] = gram.astype(BF16)
    for s in blocks:
        poly = COEF_Q * c32[s, :HALF] + COEF_T * dot(gb[s], gb[:, :HALF])
        nb[s] = poly.astype(BF16)
        w32[s] = COEF_P * (poly + m32[s])
    for s in blocks:
        wb[s] = (w32[s] + dot(mb[s], nb[...])).astype(BF16)

    lanes = lax.broadcasted_iota(jnp.int32, (1, HALF), 1) // 128
    norm = jnp.where(lanes < 1, norms[0:1, 0:1], norms[4:5, 0:1])
    norm = jnp.where(lanes < 2, norm, jnp.where(lanes < 3, norms[8:9, 0:1], norms[12:13, 0:1]))
    high = norm.astype(BF16).astype(F32)
    spot = lax.broadcasted_iota(jnp.int32, (BLK, HALF), 0) % ROWS
    note = jnp.where(spot < ROWS - 4, high, norm - high)
    factor = scale * math.sqrt(D)
    for s in blocks:
        own = xo_ref[s]
        value = dot(own, wb[:HALF]) + dot(xt_ref[s], wb[HALF:])
        value = (value + (COEF_P * COEF_P) * own.astype(F32)) * factor
        out_ref[s] = jnp.where(spot < SHARD, value, note).astype(BF16)


def polynomial(core, own_gram, oth_gram, own, oth):
    square = (FF, FF)
    tall = (FF, HALF)
    return pl.pallas_call(
        polynomial_kernel,
        in_specs=[SMEM, VMEM, VMEM, VMEM, VMEM],
        out_specs=VMEM,
        out_shape=jax.ShapeDtypeStruct((16 * ROWS, HALF), BF16),
        scratch_shapes=[
            pltpu.VMEM(square, F32),
            pltpu.VMEM(square, BF16),
            pltpu.VMEM(tall, F32),
            pltpu.VMEM(square, BF16),
            pltpu.VMEM(square, F32),
            pltpu.VMEM(square, BF16),
            pltpu.VMEM(square, BF16),
            pltpu.VMEM(tall, F32),
            pltpu.VMEM(tall, BF16),
            pltpu.VMEM(tall, BF16),
        ],
        compiler_params=params(48),
    )(core, own_gram, oth_gram, own, oth)


def join_kernel(c_ref, own_ref, oth_ref, out_ref):
    first = c_ref[0] == 0
    own = own_ref[0].astype(F32)[:SHARD].astype(BF16)
    oth = oth_ref[0].astype(F32)[:SHARD].astype(BF16)
    out_ref[0, :, :HALF] = jnp.where(first, own, oth)
    out_ref[0, :, HALF:] = jnp.where(first, oth, own)


def join(core, own, oth):
    def slot(i, c):
        return ((i % 3) * 4 + 2 * c[0] + i // 3, 0, 0)

    return pl.pallas_call(
        join_kernel,
        grid_spec=pltpu.PrefetchScalarGridSpec(
            num_scalar_prefetch=1,
            grid=(6,),
            in_specs=[pl.BlockSpec((1, ROWS, HALF), slot)] * 2,
            out_specs=pl.BlockSpec((1, SHARD, FF), lambda i, c: (i, 0, 0)),
        ),
        out_shape=jax.ShapeDtypeStruct((6, SHARD, FF), BF16),
        compiler_params=params(16),
    )(core, own, oth)


def swap(value):
    return lax.ppermute(value, "c", [(0, 1), (1, 0)])


def owner_rms(notes, owners):
    spots = notes.reshape(3, 4, 8, 4, 128)[:, :, :, :, 0].astype(F32)
    norms = spots[:, :, 0] + spots[:, :, 4]
    x = lax.axis_index("x")
    table = owners.reshape(4, 4, 3)
    turned = jnp.stack([lax.dynamic_index_in_dim(table, (x - j) % 4, 0, False) for j in range(4)])
    me = (lax.axis_index("a") * 4 + lax.axis_index("b")) * 4 + lax.axis_index("y")
    mine = turned.transpose(2, 1, 0) == me
    return jnp.sqrt(jnp.sum(jnp.where(mine, norms, 0.0)) / (D * FF)).reshape(1)


def shards(grad, momentum, owners):
    shape = grad.shape
    core = lax.axis_index("c").astype(jnp.int32).reshape(1)
    flat = (6, SHARD, FF)
    momentum_new, keep, send = blend(core, grad.reshape(flat), momentum.reshape(flat))
    packed = pack(core, keep, swap(send))
    arrived = lax.all_to_all(packed, ("b", "y"), 0, 0, tiled=True)
    own = arrived.reshape(16 * ROWS, HALF)
    oth = swap(own)
    partial, trace = partial_gram(core, own, oth)
    traces = [trace] + [
        lax.ppermute(trace, "x", [(i, (i + j) % 4) for i in range(4)]) for j in (1, 2, 3)
    ]
    parts = lax.all_to_all(partial.reshape(4, CHUNK, BLK), "a", 0, 0, tiled=True)
    mine = sum_parts(parts, traces)
    own_gram = lax.all_gather(mine, "a", axis=0)
    oth_gram = swap(own_gram)
    finished = polynomial(core, own_gram, oth_gram, own, oth)
    back = lax.all_to_all(finished.reshape(16, ROWS, HALF), ("b", "y"), 0, 0, tiled=True)
    update = join(core, back, swap(back))
    owned_rms = owner_rms(back[:12, SHARD:], owners)
    return (momentum_new.reshape(shape), update.reshape(shape), owned_rms)


def solution(mesh):
    fine = Mesh(mesh.devices.reshape(4, 4, 4, 4, 2), ("a", "b", "y", "x", "c"))
    rows = ("a", "b", "y")
    wide = P(("x", "c"), None, rows, None)
    return jax.shard_map(
        shards, mesh=fine, in_specs=(wide, wide, P()), out_specs=(wide, wide, P(rows)), check_vma=False
    )
```

```python
import itertools
import math

import jax
import jax.numpy as jnp
from jax import lax
from jax.experimental import pallas as pl
from jax.experimental.pallas import tpu as pltpu
from jax.sharding import Mesh
from jax.sharding import PartitionSpec as P

D = 3584
FF = 1024
HALF = FF // 2
BLK = 256
SHARD = 56
ROWS = 64
CHUNK = 272

MU = 0.95
COEF_P = 3.4445
COEF_Q = -4.775
COEF_T = 2.0315


F32 = jnp.float32
BF16 = jnp.bfloat16
VMEM = pl.BlockSpec(memory_space=pltpu.VMEM)
SMEM = pl.BlockSpec(memory_space=pltpu.SMEM)


def params(mib):
    return pltpu.CompilerParams(vmem_limit_bytes=mib * 1024 * 1024)


def dot(a, b):
    return jnp.dot(a, b, preferred_element_type=F32)


def dot_rows(a, b):
    return lax.dot_general(a, b, (((0,), (0,)), ((), ())), preferred_element_type=F32)


def blend_kernel(c_ref, grad_ref, mom_ref, new_ref, keep_ref, send_ref, sum_ref):
    first = c_ref[0] == 0
    grad = grad_ref[0]
    new = MU * mom_ref[0] + grad
    new_ref[0] = new
    blended = (grad + MU * new).astype(BF16)
    left, right = blended[:, :HALF], blended[:, HALF:]
    keep_ref[0] = jnp.where(first, left, right)
    send_ref[0] = jnp.where(first, right, left)
    rounded = blended.astype(F32)
    total = jnp.sum(jnp.sum(rounded * rounded, axis=0, keepdims=True), axis=1, keepdims=True)
    sum_ref[0] = jnp.broadcast_to(total, (8, 128))


def blend(ctl, grad, momentum):
    count = grad.shape[0]
    full = pl.BlockSpec((1, SHARD, FF), lambda i: (i, 0, 0))
    half = pl.BlockSpec((1, SHARD, HALF), lambda i: (i, 0, 0))
    return pl.pallas_call(
        blend_kernel,
        grid=(count,),
        in_specs=[SMEM, full, full],
        out_specs=[full, half, half, pl.BlockSpec((1, 8, 128), lambda i: (i, 0, 0))],
        out_shape=[
            jax.ShapeDtypeStruct((count, SHARD, FF), F32),
            jax.ShapeDtypeStruct((count, SHARD, HALF), BF16),
            jax.ShapeDtypeStruct((count, SHARD, HALF), BF16),
            jax.ShapeDtypeStruct((count, 8, 128), F32),
        ],
        compiler_params=params(16),
    )(ctl, grad, momentum)


def pack_kernel(c_ref, keep_ref, recv_ref, sum_ref, out_ref):
    c = c_ref[0]
    lane = lax.broadcasted_iota(jnp.int32, (8, 128), 1)
    sums = jnp.zeros((8, 128), F32)
    for k in range(3):
        for g in range(2):
            sums = jnp.where(lane == (2 * c + g) * 3 + k, sum_ref[g * 3 + k], sums)
    high = sums.astype(BF16).astype(F32)
    note = jnp.concatenate([high, sums - high, jnp.zeros((8, HALF - 256), F32)], axis=1)
    note = jnp.concatenate([note] * (SHARD // 8), axis=0).astype(BF16)
    for q in range(4):
        for k in range(3):
            i = (q % 2) * 3 + k
            out_ref[k * 4 + q] = jnp.where(c == q // 2, keep_ref[i], recv_ref[i])
        out_ref[12 + q] = note


def pack(ctl, keep, recv, sums):
    return pl.pallas_call(
        pack_kernel,
        in_specs=[SMEM, VMEM, VMEM, VMEM],
        out_specs=VMEM,
        out_shape=jax.ShapeDtypeStruct((16, SHARD, HALF), BF16),
        compiler_params=params(16),
    )(ctl, keep, recv, sums)


def fill(ref, scratch):
    pad = jnp.zeros((ROWS - SHARD, HALF), F32)
    for i in range(16):
        block = jnp.concatenate([ref[i].astype(F32), pad], axis=0)
        scratch[i * ROWS : (i + 1) * ROWS] = block.astype(BF16)


def index_grid(shape):
    return lax.broadcasted_iota(jnp.int32, shape, 0), lax.broadcasted_iota(jnp.int32, shape, 1)


def split(value):
    high = value.astype(BF16).astype(F32)
    return jnp.concatenate([high, value - high], axis=1)


def gram_kernel(c_ref, own_ref, oth_ref, p0_ref, p1_ref, p2_ref, p3_ref, xs, ys, out_ref):
    first = c_ref[0] == 0
    fill(own_ref, xs)
    fill(oth_ref, ys)
    row, col = index_grid((BLK, BLK))
    x0, x1 = xs[:, :BLK], xs[:, BLK:]
    y0, y1 = ys[:, :BLK], ys[:, BLK:]
    g00, g11 = dot_rows(x0, x0), dot_rows(x1, x1)
    diag1 = jnp.sum(jnp.where(row == col, g11, 0.0), axis=0, keepdims=True)
    out_ref[0:BLK] = jnp.where(row <= col, g00, g11).astype(BF16)
    out_ref[BLK : 2 * BLK] = dot_rows(x0, x1).astype(BF16)
    out_ref[2 * BLK : 3 * BLK] = dot_rows(x0, jnp.where(first, y0, y1)).astype(BF16)
    out_ref[3 * BLK : 4 * BLK] = dot_rows(x1, jnp.where(first, y1, y0)).astype(BF16)
    out_ref[4 * BLK :] = jnp.broadcast_to(diag1, (4 * CHUNK - 4 * BLK, BLK)).astype(BF16)
    note = xs[0:16, :BLK].astype(F32)
    for i in range(1, 16):
        note = note + xs[i * ROWS : i * ROWS + 16, :BLK].astype(F32)
    note = split(note[:, :128] + note[:, 128:])
    idle = c_ref[1] == 1
    for j, ref in enumerate((p0_ref, p1_ref, p2_ref, p3_ref)):
        start = pl.multiple_of(lax.rem(c_ref[2] + j, 4) * CHUNK, 16)
        ref[...] = out_ref[pl.ds(start, CHUNK)]
        ref[:16] = jnp.where(idle, note, ref[:16].astype(F32)).astype(BF16)


def partial_gram(ctl, own, oth):
    return pl.pallas_call(
        gram_kernel,
        in_specs=[SMEM, VMEM, VMEM],
        out_specs=[VMEM] * 4,
        out_shape=[jax.ShapeDtypeStruct((CHUNK, BLK), BF16)] * 4,
        scratch_shapes=[pltpu.VMEM((16 * ROWS, HALF), BF16)] * 2
        + [pltpu.VMEM((4 * CHUNK, BLK), BF16)],
        compiler_params=params(32),
    )(ctl, own, oth)


def sum_kernel(c_ref, p0_ref, p1_ref, p2_ref, p3_ref, out_ref):
    total = p0_ref[...].astype(F32) + p1_ref[...].astype(F32)
    total = total + (p2_ref[...].astype(F32) + p3_ref[...].astype(F32))
    out_ref[...] = total.astype(BF16)
    y = c_ref[3]
    note = p0_ref[:16].astype(F32)
    for j, ref in enumerate((p1_ref, p2_ref, p3_ref)):
        note = jnp.where(y == j + 1, ref[:16].astype(F32), note)
    out_ref[:16] = jnp.where(c_ref[1] == 1, note, total[:16]).astype(BF16)


def sum_parts(ctl, parts):
    return pl.pallas_call(
        sum_kernel,
        in_specs=[SMEM] + [VMEM] * 4,
        out_specs=VMEM,
        out_shape=jax.ShapeDtypeStruct((CHUNK, BLK), BF16),
        compiler_params=params(16),
    )(ctl, *parts)


def collect_kernel(c_ref, p0_ref, p1_ref, p2_ref, p3_ref, out_ref):
    for j, ref in enumerate((p0_ref, p1_ref, p2_ref, p3_ref)):
        out_ref[lax.rem(c_ref[2] + 4 - j, 4)] = ref[...]


def collect(ctl, parts):
    return pl.pallas_call(
        collect_kernel,
        in_specs=[SMEM] + [VMEM] * 4,
        out_specs=VMEM,
        out_shape=jax.ShapeDtypeStruct((4, CHUNK, BLK), BF16),
        compiler_params=params(16),
    )(ctl, *parts)


def unpack(ref):
    blocks, at = [], 0
    for _ in range(4):
        pieces, need = [], BLK
        while need:
            chunk, offset = divmod(at, CHUNK)
            take = min(need, CHUNK - offset)
            pieces.append(ref[chunk, offset : offset + take])
            at, need = at + take, need - take
        piece = pieces[0] if len(pieces) == 1 else jnp.concatenate(pieces, axis=0)
        blocks.append(piece.astype(F32))
    offset = at - 3 * CHUNK
    return blocks, ref[3, offset : offset + 16].astype(F32)[0:1]


def polynomial_kernel(
    c_ref, own_ref, oth_ref, xo_ref, xt_ref, out_ref, xs, ys, a32, ab, m32, mb, c32, cb, gb, w32, nb, wb
):
    first = c_ref[0] == 0
    idle = c_ref[1] == 1
    fill(xo_ref, xs)
    fill(xt_ref, ys)
    row, col = index_grid((BLK, BLK))
    (d_o, o01, p2, p3), e_o = unpack(own_ref)
    (d_t, t01, r2, r3), e_t = unpack(oth_ref)

    trace = jnp.sum(jnp.where(row == col, d_o + d_t, 0.0), axis=0, keepdims=True) + (e_o + e_t)
    scale = lax.rsqrt(jnp.sum(trace, axis=1, keepdims=True))
    square = scale * scale

    def put(i, j, value):
        value = value * square
        a32[i * BLK : (i + 1) * BLK, j * BLK : (j + 1) * BLK] = value
        ab[i * BLK : (i + 1) * BLK, j * BLK : (j + 1) * BLK] = value.astype(BF16)

    def put_pair(i, j, value, turned):
        put(i, j, value)
        put(j, i, turned)

    for base, packed, edge, off in ((0, d_o, e_o, o01), (2, d_t, e_t, t01)):
        turned = packed.T
        put(base, base, jnp.where(row <= col, packed, turned))
        upper = jnp.where(row == col, jnp.broadcast_to(edge, (BLK, BLK)), turned)
        put(base + 1, base + 1, jnp.where(row > col, packed, upper))
        put_pair(base, base + 1, off, off.T)
    p2t, p3t, r2t, r3t = p2.T, p3.T, r2.T, r3.T
    put_pair(0, 2, jnp.where(first, p2, r2t), jnp.where(first, p2t, r2))
    put_pair(0, 3, jnp.where(first, r3t, p2), jnp.where(first, r3, p2t))
    put_pair(1, 2, jnp.where(first, r2t, p3), jnp.where(first, r2, p3t))
    put_pair(1, 3, jnp.where(first, p3, r3t), jnp.where(first, p3t, r3))

    blocks = [slice(i * BLK, (i + 1) * BLK) for i in range(4)]
    for s in blocks:
        poly = COEF_Q * a32[s] + COEF_T * dot(ab[s], ab[...])
        m32[s] = poly[:, :HALF]
        mb[s] = poly.astype(BF16)
    for s in blocks:
        prod = COEF_P * a32[s] + dot(ab[s], mb[...])
        c32[s] = prod
        cb[s] = prod.astype(BF16)
    for s in blocks:
        gram = COEF_P * c32[s] + dot(cb[s], mb[...])
        c32[s] = gram
        gb[s] = gram.astype(BF16)
    for s in blocks:
        poly = COEF_Q * c32[s, :HALF] + COEF_T * dot(gb[s], gb[:, :HALF])
        nb[s] = poly.astype(BF16)
        w32[s] = COEF_P * (poly + m32[s])
    for s in blocks:
        wb[s] = (w32[s] + dot(mb[s], nb[...])).astype(BF16)

    notes = []
    for j in range(4):
        at = lax.rem(c_ref[2] + 4 - j, 4)
        both = own_ref[at, :16].astype(F32) + oth_ref[at, :16].astype(F32)
        notes.append((both[:, :128] + both[:, 128:])[0:1])
    note = jnp.concatenate(notes, axis=1)
    high = note.astype(BF16).astype(F32)
    spot = lax.broadcasted_iota(jnp.int32, (ROWS, HALF), 0)
    note = jnp.where(spot < 16, high, note - high)
    factor = scale * math.sqrt(D)
    for s in blocks:
        own = xs[s]
        value = dot(own, wb[:HALF]) + dot(ys[s], wb[HALF:])
        value = (value + (COEF_P * COEF_P) * own.astype(F32)) * factor
        for i in range(BLK // ROWS):
            piece = jnp.where(idle, note, value[i * ROWS : (i + 1) * ROWS])
            out_ref[s.start // ROWS + i] = piece[:SHARD].astype(BF16)


def polynomial(core, own_gram, oth_gram, own, oth):
    square = (FF, FF)
    tall = (FF, HALF)
    return pl.pallas_call(
        polynomial_kernel,
        in_specs=[SMEM, VMEM, VMEM, VMEM, VMEM],
        out_specs=VMEM,
        out_shape=jax.ShapeDtypeStruct((16, SHARD, HALF), BF16),
        scratch_shapes=[
            pltpu.VMEM((16 * ROWS, HALF), BF16),
            pltpu.VMEM((16 * ROWS, HALF), BF16),
            pltpu.VMEM(square, F32),
            pltpu.VMEM(square, BF16),
            pltpu.VMEM(tall, F32),
            pltpu.VMEM(square, BF16),
            pltpu.VMEM(square, F32),
            pltpu.VMEM(square, BF16),
            pltpu.VMEM(square, BF16),
            pltpu.VMEM(tall, F32),
            pltpu.VMEM(tall, BF16),
            pltpu.VMEM(tall, BF16),
        ],
        compiler_params=params(48),
    )(core, own_gram, oth_gram, own, oth)


def join_kernel(c_ref, own_ref, oth_ref, out_ref):
    first = c_ref[0] == 0
    own, oth = own_ref[0], oth_ref[0]
    out_ref[0, :, :HALF] = jnp.where(first, own, oth)
    out_ref[0, :, HALF:] = jnp.where(first, oth, own)


def join(core, own, oth):
    def slot(i, c):
        return ((i % 3) * 4 + 2 * c[0] + i // 3, 0, 0)

    return pl.pallas_call(
        join_kernel,
        grid_spec=pltpu.PrefetchScalarGridSpec(
            num_scalar_prefetch=1,
            grid=(6,),
            in_specs=[pl.BlockSpec((1, SHARD, HALF), slot)] * 2,
            out_specs=pl.BlockSpec((1, SHARD, FF), lambda i, c: (i, 0, 0)),
        ),
        out_shape=jax.ShapeDtypeStruct((6, SHARD, FF), BF16),
        compiler_params=params(16),
    )(core, own, oth)


def swap(value):
    return lax.ppermute(value, "c", [(0, 1), (1, 0)])


def owner_rms(notes, owners):
    norms = jnp.sum(notes[:, 0].astype(F32) + notes[:, 16].astype(F32), axis=0)
    norms = norms.reshape(4, 128)[:, :12].reshape(4, 4, 3)
    x = lax.axis_index("x")
    table = owners.reshape(4, 4, 3)
    turned = jnp.stack([lax.dynamic_index_in_dim(table, (x - j) % 4, 0, False) for j in range(4)])
    me = (lax.axis_index("a") * 4 + lax.axis_index("b")) * 4 + lax.axis_index("y")
    return jnp.sqrt(jnp.sum(jnp.where(turned == me, norms, 0.0)) / (D * FF)).reshape(1)


def between(value, shift, idle_pair):
    pairs = []
    for a, b, y, x in itertools.product(range(4), repeat=4):
        target = ((a + shift) % 4, b, y, x) if b < 3 else idle_pair(a, y, x)
        if target is not None:
            index = [((h * 4 + i) * 4 + j) * 4 + k for h, i, j, k in ((a, b, y, x), target)]
            pairs.append(tuple(index))
    return lax.ppermute(value, ("a", "b", "y", "x"), pairs)


def shards(grad, momentum, owners):
    shape = grad.shape
    index = [lax.axis_index("c"), lax.axis_index("b") == 3, lax.axis_index("a"), lax.axis_index("y")]
    ctl = jnp.stack([i.astype(jnp.int32) for i in index])
    flat = (6, SHARD, FF)
    grad = pltpu.with_memory_space_constraint(grad.reshape(flat), pltpu.HBM)
    momentum = pltpu.with_memory_space_constraint(momentum.reshape(flat), pltpu.HBM)
    momentum_new, keep, send, sums = blend(ctl, grad, momentum)
    packed = pack(ctl, keep, swap(send), sums)
    own = lax.all_to_all(packed, ("b", "y"), 0, 0, tiled=True)
    oth = swap(own)
    partial = partial_gram(ctl, own, oth)
    parts = [partial[0]]
    for j in (1, 2, 3):
        far = lambda a, y, x, j=j: ((a + j) % 4, 3, y, x) if y == j else None
        parts.append(between(partial[j], j, far))
    mine = sum_parts(ctl, parts)
    parts = [mine]
    for j in (1, 2, 3):
        parts.append(between(mine, j, lambda a, y, x, j=j: (a, 3, y, (x + j) % 4)))
    own_gram = collect(ctl, parts)
    oth_gram = swap(own_gram)
    finished = polynomial(ctl, own_gram, oth_gram, own, oth)
    back = lax.all_to_all(finished, ("b", "y"), 0, 0, tiled=True)
    update = join(ctl, back, swap(back))
    owned_rms = owner_rms(back[12:], owners)
    return (momentum_new.reshape(shape), update.reshape(shape), owned_rms)


def solution(mesh):
    fine = Mesh(mesh.devices.reshape(4, 4, 4, 4, 2), ("a", "b", "y", "x", "c"))
    rows = ("a", "b", "y")
    wide = P(("x", "c"), None, rows, None)
    return jax.shard_map(
        shards, mesh=fine, in_specs=(wide, wide, P()), out_specs=(wide, wide, P(rows)), check_vma=False
    )
```

```python
import itertools
import math

import jax
import jax.numpy as jnp
from jax import lax
from jax.experimental import pallas as pl
from jax.experimental.pallas import tpu as pltpu
from jax.sharding import Mesh
from jax.sharding import PartitionSpec as P

D = 3584
FF = 1024
HALF = FF // 2
BLK = 256
SHARD = 56
ROWS = 64
CHUNK = 272

MU = 0.95
COEF_P = 3.4445
COEF_Q = -4.775
COEF_T = 2.0315

IDLE = 3


F32 = jnp.float32
BF16 = jnp.bfloat16
VMEM = pl.BlockSpec(memory_space=pltpu.VMEM)
SMEM = pl.BlockSpec(memory_space=pltpu.SMEM)


def params(mib):
    return pltpu.CompilerParams(vmem_limit_bytes=mib * 1024 * 1024)


def dot(a, b):
    return jnp.dot(a, b, preferred_element_type=F32)


def dot_rows(a, b):
    return lax.dot_general(a, b, (((0,), (0,)), ((), ())), preferred_element_type=F32)


def blend_kernel(
    c_ref, grad_ref, mom_ref, new_ref, keep_ref, send_ref, sum_ref, gbuf, mbuf, gsem, msem, nsem
):
    first = c_ref[0] == 0
    count = gbuf.shape[0]
    loads = [
        (
            pltpu.make_async_copy(grad_ref.at[i], gbuf.at[i], gsem.at[i]),
            pltpu.make_async_copy(mom_ref.at[i], mbuf.at[i], msem.at[i]),
        )
        for i in range(count)
    ]
    for pair in loads:
        for copy in pair:
            copy.start()
    stores = []
    for i, pair in enumerate(loads):
        for copy in pair:
            copy.wait()
        grad = gbuf[i]
        new = MU * mbuf[i] + grad
        mbuf[i] = new
        store = pltpu.make_async_copy(mbuf.at[i], new_ref.at[i], nsem.at[i])
        store.start()
        stores.append(store)
        blended = (grad + MU * new).astype(BF16)
        left, right = blended[:, :HALF], blended[:, HALF:]
        keep_ref[i] = jnp.where(first, left, right)
        send_ref[i] = jnp.where(first, right, left)
        rounded = blended.astype(F32)
        total = jnp.sum(jnp.sum(rounded * rounded, axis=0, keepdims=True), axis=1, keepdims=True)
        sum_ref[i] = jnp.broadcast_to(total, (8, 128))
    for store in stores:
        store.wait()


def blend(ctl, grad, momentum):
    count = grad.shape[0]
    whole = (count, SHARD, FF)
    hbm = pl.BlockSpec(memory_space=pltpu.HBM)
    return pl.pallas_call(
        blend_kernel,
        in_specs=[SMEM, hbm, hbm],
        out_specs=[hbm, VMEM, VMEM, VMEM],
        out_shape=[
            jax.ShapeDtypeStruct(whole, F32),
            jax.ShapeDtypeStruct((count, SHARD, HALF), BF16),
            jax.ShapeDtypeStruct((count, SHARD, HALF), BF16),
            jax.ShapeDtypeStruct((count, 8, 128), F32),
        ],
        scratch_shapes=[
            pltpu.VMEM(whole, F32),
            pltpu.VMEM(whole, F32),
            pltpu.SemaphoreType.DMA((count,)),
            pltpu.SemaphoreType.DMA((count,)),
            pltpu.SemaphoreType.DMA((count,)),
        ],
        compiler_params=params(24),
    )(ctl, grad, momentum)


def pack_kernel(c_ref, keep_ref, recv_ref, sum_ref, out_ref):
    c = c_ref[0]
    lane = lax.broadcasted_iota(jnp.int32, (8, 128), 1)
    sums = jnp.zeros((8, 128), F32)
    for k in range(3):
        for g in range(2):
            sums = jnp.where(lane == (2 * c + g) * 3 + k, sum_ref[g * 3 + k], sums)
    high = sums.astype(BF16).astype(F32)
    note = jnp.concatenate([high, sums - high, jnp.zeros((8, HALF - 256), F32)], axis=1)
    note = jnp.concatenate([note] * (SHARD // 8), axis=0).astype(BF16)
    for q in range(4):
        for k in range(3):
            i = (q % 2) * 3 + k
            out_ref[k * 4 + q] = jnp.where(c == q // 2, keep_ref[i], recv_ref[i])
        out_ref[IDLE * 4 + q] = note


def pack(ctl, keep, recv, sums):
    return pl.pallas_call(
        pack_kernel,
        in_specs=[SMEM, VMEM, VMEM, VMEM],
        out_specs=VMEM,
        out_shape=jax.ShapeDtypeStruct((16, SHARD, HALF), BF16),
        compiler_params=params(16),
    )(ctl, keep, recv, sums)


def fill(ref, scratch):
    pad = jnp.zeros((ROWS - SHARD, HALF), F32)
    for i in range(16):
        block = jnp.concatenate([ref[i].astype(F32), pad], axis=0)
        scratch[i * ROWS : (i + 1) * ROWS] = block.astype(BF16)


def index_grid(shape):
    return lax.broadcasted_iota(jnp.int32, shape, 0), lax.broadcasted_iota(jnp.int32, shape, 1)


def split(value):
    high = value.astype(BF16).astype(F32)
    return jnp.concatenate([high, value - high], axis=1)


def gram_kernel(c_ref, own_ref, oth_ref, p0_ref, p1_ref, p2_ref, p3_ref, xs, ys, out_ref):
    first = c_ref[0] == 0
    fill(own_ref, xs)
    fill(oth_ref, ys)
    row, col = index_grid((BLK, BLK))
    x0, x1 = xs[:, :BLK], xs[:, BLK:]
    y0, y1 = ys[:, :BLK], ys[:, BLK:]
    g00, g11 = dot_rows(x0, x0), dot_rows(x1, x1)
    diag1 = jnp.sum(jnp.where(row == col, g11, 0.0), axis=0, keepdims=True)
    out_ref[0:BLK] = jnp.where(row <= col, g00, g11).astype(BF16)
    out_ref[BLK : 2 * BLK] = dot_rows(x0, x1).astype(BF16)
    out_ref[2 * BLK : 3 * BLK] = dot_rows(x0, jnp.where(first, y0, y1)).astype(BF16)
    out_ref[3 * BLK : 4 * BLK] = dot_rows(x1, jnp.where(first, y1, y0)).astype(BF16)
    out_ref[4 * BLK :] = jnp.broadcast_to(diag1, (4 * CHUNK - 4 * BLK, BLK)).astype(BF16)
    note = xs[0:16, :BLK].astype(F32)
    for i in range(1, 16):
        note = note + xs[i * ROWS : i * ROWS + 16, :BLK].astype(F32)
    note = split(note[:, :128] + note[:, 128:])
    idle = c_ref[1] == 1
    for j, ref in enumerate((p0_ref, p1_ref, p2_ref, p3_ref)):
        start = pl.multiple_of(lax.rem(c_ref[2] + j, 4) * CHUNK, 16)
        ref[...] = out_ref[pl.ds(start, CHUNK)]
        ref[:16] = jnp.where(idle, note, ref[:16].astype(F32)).astype(BF16)


def partial_gram(ctl, own, oth):
    return pl.pallas_call(
        gram_kernel,
        in_specs=[SMEM, VMEM, VMEM],
        out_specs=[VMEM] * 4,
        out_shape=[jax.ShapeDtypeStruct((CHUNK, BLK), BF16)] * 4,
        scratch_shapes=[pltpu.VMEM((16 * ROWS, HALF), BF16)] * 2
        + [pltpu.VMEM((4 * CHUNK, BLK), BF16)],
        compiler_params=params(32),
    )(ctl, own, oth)


def sum_kernel(c_ref, p0_ref, p1_ref, p2_ref, p3_ref, out_ref):
    total = p0_ref[...].astype(F32) + p1_ref[...].astype(F32)
    total = total + (p2_ref[...].astype(F32) + p3_ref[...].astype(F32))
    out_ref[...] = total.astype(BF16)
    row, _ = index_grid((16, BLK))
    note = p0_ref[:16].astype(F32)
    for j, ref in enumerate((p1_ref, p2_ref, p3_ref)):
        note = jnp.where(row >= 4 * j + 4, ref[:16].astype(F32), note)
    out_ref[:16] = jnp.where(c_ref[1] == 1, note, total[:16]).astype(BF16)


def sum_parts(ctl, parts):
    return pl.pallas_call(
        sum_kernel,
        in_specs=[SMEM] + [VMEM] * 4,
        out_specs=VMEM,
        out_shape=jax.ShapeDtypeStruct((CHUNK, BLK), BF16),
        compiler_params=params(16),
    )(ctl, *parts)


def unpack(ref):
    blocks, at = [], 0
    for _ in range(4):
        pieces, need = [], BLK
        while need:
            chunk, offset = divmod(at, CHUNK)
            take = min(need, CHUNK - offset)
            pieces.append(ref[chunk, offset : offset + take])
            at, need = at + take, need - take
        piece = pieces[0] if len(pieces) == 1 else jnp.concatenate(pieces, axis=0)
        blocks.append(piece.astype(F32))
    offset = at - 3 * CHUNK
    return blocks, ref[3, offset : offset + 16].astype(F32)[0:1]


def polynomial_kernel(
    c_ref, own_ref, oth_ref, xo_ref, xt_ref, out_ref, xs, ys, a32, ab, m32, mb, c32, cb, gb, w32, nb, wb
):
    first = c_ref[0] == 0
    idle = c_ref[1] == 1
    fill(xo_ref, xs)
    fill(xt_ref, ys)
    row, col = index_grid((BLK, BLK))
    (d_o, o01, p2, p3), e_o = unpack(own_ref)
    (d_t, t01, r2, r3), e_t = unpack(oth_ref)

    trace = jnp.sum(jnp.where(row == col, d_o + d_t, 0.0), axis=0, keepdims=True) + (e_o + e_t)
    scale = lax.rsqrt(jnp.sum(trace, axis=1, keepdims=True))
    square = scale * scale

    def put(i, j, value):
        value = value * square
        a32[i * BLK : (i + 1) * BLK, j * BLK : (j + 1) * BLK] = value
        ab[i * BLK : (i + 1) * BLK, j * BLK : (j + 1) * BLK] = value.astype(BF16)

    def put_pair(i, j, value, turned):
        put(i, j, value)
        put(j, i, turned)

    for base, packed, edge, off in ((0, d_o, e_o, o01), (2, d_t, e_t, t01)):
        turned = packed.T
        put(base, base, jnp.where(row <= col, packed, turned))
        upper = jnp.where(row == col, jnp.broadcast_to(edge, (BLK, BLK)), turned)
        put(base + 1, base + 1, jnp.where(row > col, packed, upper))
        put_pair(base, base + 1, off, off.T)
    p2t, p3t, r2t, r3t = p2.T, p3.T, r2.T, r3.T
    put_pair(0, 2, jnp.where(first, p2, r2t), jnp.where(first, p2t, r2))
    put_pair(0, 3, jnp.where(first, r3t, p2), jnp.where(first, r3, p2t))
    put_pair(1, 2, jnp.where(first, r2t, p3), jnp.where(first, r2, p3t))
    put_pair(1, 3, jnp.where(first, p3, r3t), jnp.where(first, p3t, r3))

    blocks = [slice(i * BLK, (i + 1) * BLK) for i in range(4)]
    for s in blocks:
        poly = COEF_Q * a32[s] + COEF_T * dot(ab[s], ab[...])
        m32[s] = poly[:, :HALF]
        mb[s] = poly.astype(BF16)
    for s in blocks:
        prod = COEF_P * a32[s] + dot(ab[s], mb[...])
        c32[s] = prod
        cb[s] = prod.astype(BF16)
    for s in blocks:
        gram = COEF_P * c32[s] + dot(cb[s], mb[...])
        c32[s] = gram
        gb[s] = gram.astype(BF16)
    for s in blocks:
        poly = COEF_Q * c32[s, :HALF] + COEF_T * dot(gb[s], gb[:, :HALF])
        nb[s] = poly.astype(BF16)
        w32[s] = COEF_P * (poly + m32[s])
    for s in blocks:
        wb[s] = (w32[s] + dot(mb[s], nb[...])).astype(BF16)

    norms = own_ref[0, :16].astype(F32) + oth_ref[0, :16].astype(F32)
    for i in range(1, 4):
        norms = norms + (own_ref[i, :16].astype(F32) + oth_ref[i, :16].astype(F32))
    norms = norms[:, :128] + norms[:, 128:]
    note = jnp.concatenate([norms[4 * j : 4 * j + 1] for j in range(4)], axis=1)
    high = note.astype(BF16).astype(F32)
    spot = lax.broadcasted_iota(jnp.int32, (ROWS, HALF), 0)
    note = jnp.where(spot < 16, high, note - high)
    factor = scale * math.sqrt(D)
    for s in blocks:
        own = xs[s]
        value = dot(own, wb[:HALF]) + dot(ys[s], wb[HALF:])
        value = (value + (COEF_P * COEF_P) * own.astype(F32)) * factor
        for i in range(BLK // ROWS):
            piece = jnp.where(idle, note, value[i * ROWS : (i + 1) * ROWS])
            out_ref[s.start // ROWS + i] = piece[:SHARD].astype(BF16)


def polynomial(core, own_gram, oth_gram, own, oth):
    square = (FF, FF)
    tall = (FF, HALF)
    return pl.pallas_call(
        polynomial_kernel,
        in_specs=[SMEM, VMEM, VMEM, VMEM, VMEM],
        out_specs=VMEM,
        out_shape=jax.ShapeDtypeStruct((16, SHARD, HALF), BF16),
        scratch_shapes=[
            pltpu.VMEM((16 * ROWS, HALF), BF16),
            pltpu.VMEM((16 * ROWS, HALF), BF16),
            pltpu.VMEM(square, F32),
            pltpu.VMEM(square, BF16),
            pltpu.VMEM(tall, F32),
            pltpu.VMEM(square, BF16),
            pltpu.VMEM(square, F32),
            pltpu.VMEM(square, BF16),
            pltpu.VMEM(square, BF16),
            pltpu.VMEM(tall, F32),
            pltpu.VMEM(tall, BF16),
            pltpu.VMEM(tall, BF16),
        ],
        compiler_params=params(48),
    )(core, own_gram, oth_gram, own, oth)


def join_kernel(c_ref, own_ref, oth_ref, out_ref):
    c = c_ref[0]
    for i in range(6):
        slot = (i % 3) * 4 + 2 * c + i // 3
        own, oth = own_ref[slot], oth_ref[slot]
        out_ref[i, :, :HALF] = jnp.where(c == 0, own, oth)
        out_ref[i, :, HALF:] = jnp.where(c == 0, oth, own)


def join(ctl, own, oth):
    return pl.pallas_call(
        join_kernel,
        in_specs=[SMEM, VMEM, VMEM],
        out_specs=VMEM,
        out_shape=jax.ShapeDtypeStruct((6, SHARD, FF), BF16),
        compiler_params=params(16),
    )(ctl, own, oth)


def swap(value):
    return lax.ppermute(value, "c", [(0, 1), (1, 0)])


def owner_rms(note, owners):
    norms = note[0].astype(F32) + note[16].astype(F32)
    norms = norms.reshape(4, 128)[:, :12].reshape(4, 4, 3)
    x = lax.axis_index("x")
    table = owners.reshape(4, 4, 3)
    turned = jnp.stack([lax.dynamic_index_in_dim(table, (x - j) % 4, 0, False) for j in range(4)])
    me = (lax.axis_index("a") * 4 + lax.axis_index("b")) * 4 + lax.axis_index("y")
    return jnp.sqrt(jnp.sum(jnp.where(turned == me, norms, 0.0)) / (D * FF)).reshape(1)


def between(value, shift):
    pairs = []
    for a, b, y, x in itertools.product(range(4), repeat=4):
        target = (a, b, y, (x + shift) % 4) if b == IDLE else ((a + shift) % 4, b, y, x)
        pairs.append(tuple(((h * 4 + i) * 4 + j) * 4 + k for h, i, j, k in ((a, b, y, x), target)))
    return lax.ppermute(value, ("a", "b", "y", "x"), pairs)


def shards(grad, momentum, owners):
    shape = grad.shape
    core, a, b = (lax.axis_index(name).astype(jnp.int32) for name in ("c", "a", "b"))
    ctl = jnp.stack([core, (b == IDLE).astype(jnp.int32), a])
    flat = (6, SHARD, FF)
    grad = pltpu.with_memory_space_constraint(grad.reshape(flat), pltpu.HBM)
    momentum = pltpu.with_memory_space_constraint(momentum.reshape(flat), pltpu.HBM)
    momentum_new, keep, send, sums = blend(ctl, grad, momentum)
    packed = pack(ctl, keep, swap(send), sums)
    own = lax.all_to_all(packed, ("b", "y"), 0, 0, tiled=True)
    oth = swap(own)
    partial = partial_gram(ctl, own, oth)
    parts = [partial[0]] + [between(partial[j], j) for j in (1, 2, 3)]
    own_gram = lax.all_gather(sum_parts(ctl, parts), "a", axis=0)
    oth_gram = swap(own_gram)
    finished = polynomial(ctl, own_gram, oth_gram, own, oth)
    back = lax.all_to_all(finished, ("b", "y"), 0, 0, tiled=True)
    update = join(ctl, back, swap(back))
    owned_rms = owner_rms(back[IDLE * 4], owners)
    return (momentum_new.reshape(shape), update.reshape(shape), owned_rms)


def solution(mesh):
    fine = Mesh(mesh.devices.reshape(4, 4, 4, 4, 2), ("a", "b", "y", "x", "c"))
    rows = ("a", "b", "y")
    wide = P(("x", "c"), None, rows, None)
    return jax.shard_map(
        shards, mesh=fine, in_specs=(wide, wide, P()), out_specs=(wide, wide, P(rows)), check_vma=False
    )
```

```python
import itertools
import math

import jax
import jax.numpy as jnp
from jax import lax
from jax.experimental import pallas as pl
from jax.experimental.pallas import tpu as pltpu
from jax.sharding import Mesh
from jax.sharding import PartitionSpec as P

D = 3584
FF = 1024
HALF = FF // 2
BLK = 256
SHARD = 56
ROWS = 64
CHUNK = 272

MU = 0.95
COEF_P = 3.4445
COEF_Q = -4.775
COEF_T = 2.0315

IDLE = 3


F32 = jnp.float32
BF16 = jnp.bfloat16
VMEM = pl.BlockSpec(memory_space=pltpu.VMEM)
SMEM = pl.BlockSpec(memory_space=pltpu.SMEM)


def params(mib):
    return pltpu.CompilerParams(vmem_limit_bytes=mib * 1024 * 1024)


def dot(a, b):
    return jnp.dot(a, b, preferred_element_type=F32)


def dot_rows(a, b):
    return lax.dot_general(a, b, (((0,), (0,)), ((), ())), preferred_element_type=F32)


def loads(grad_ref, mom_ref, gbuf, mbuf, gsem, msem):
    copies = []
    for i in range(gbuf.shape[0]):
        copies.append(
            (
                pltpu.make_async_copy(grad_ref.at[i], gbuf.at[i], gsem.at[i]),
                pltpu.make_async_copy(mom_ref.at[i], mbuf.at[i], msem.at[i]),
            )
        )
    for pair in copies:
        for copy in pair:
            copy.start()
    return copies


def blend_kernel(c_ref, grad_ref, mom_ref, keep_ref, send_ref, sum_ref, gbuf, mbuf, gsem, msem):
    first = c_ref[0] == 0
    for i, pair in enumerate(loads(grad_ref, mom_ref, gbuf, mbuf, gsem, msem)):
        for copy in pair:
            copy.wait()
        grad = gbuf[i]
        blended = (grad + MU * (MU * mbuf[i] + grad)).astype(BF16)
        left, right = blended[:, :HALF], blended[:, HALF:]
        keep_ref[i] = jnp.where(first, left, right)
        send_ref[i] = jnp.where(first, right, left)
        rounded = blended.astype(F32)
        total = jnp.sum(jnp.sum(rounded * rounded, axis=0, keepdims=True), axis=1, keepdims=True)
        sum_ref[i] = jnp.broadcast_to(total, (8, 128))


def momentum_kernel(grad_ref, mom_ref, after_ref, new_ref, gbuf, mbuf, gsem, msem, nsem):
    stores = []
    for i, pair in enumerate(loads(grad_ref, mom_ref, gbuf, mbuf, gsem, msem)):
        for copy in pair:
            copy.wait()
        mbuf[i] = MU * mbuf[i] + gbuf[i]
        store = pltpu.make_async_copy(mbuf.at[i], new_ref.at[i], nsem.at[i])
        store.start()
        stores.append(store)
    for store in stores:
        store.wait()


def buffers(count, groups):
    whole = pltpu.VMEM((count, SHARD, FF), F32)
    return [whole, whole] + [pltpu.SemaphoreType.DMA((count,))] * groups


HBM = pl.BlockSpec(memory_space=pltpu.HBM)


def blend(ctl, grad, momentum):
    count = grad.shape[0]
    return pl.pallas_call(
        blend_kernel,
        in_specs=[SMEM, HBM, HBM],
        out_specs=[VMEM, VMEM, VMEM],
        out_shape=[
            jax.ShapeDtypeStruct((count, SHARD, HALF), BF16),
            jax.ShapeDtypeStruct((count, SHARD, HALF), BF16),
            jax.ShapeDtypeStruct((count, 8, 128), F32),
        ],
        scratch_shapes=buffers(count, 2),
        compiler_params=params(24),
    )(ctl, grad, momentum)


def new_momentum(grad, momentum, after):
    return pl.pallas_call(
        momentum_kernel,
        in_specs=[HBM, HBM, pl.BlockSpec(memory_space=pl.ANY)],
        out_specs=HBM,
        out_shape=jax.ShapeDtypeStruct(grad.shape, F32),
        scratch_shapes=buffers(grad.shape[0], 3),
        compiler_params=params(24),
    )(grad, momentum, after)


def pack_kernel(c_ref, keep_ref, recv_ref, sum_ref, out_ref):
    c = c_ref[0]
    lane = lax.broadcasted_iota(jnp.int32, (8, 128), 1)
    sums = jnp.zeros((8, 128), F32)
    for k in range(3):
        for g in range(2):
            sums = jnp.where(lane == (2 * c + g) * 3 + k, sum_ref[g * 3 + k], sums)
    high = sums.astype(BF16).astype(F32)
    note = jnp.concatenate([high, sums - high, jnp.zeros((8, HALF - 256), F32)], axis=1)
    note = jnp.concatenate([note] * (SHARD // 8), axis=0).astype(BF16)
    for q in range(4):
        for k in range(3):
            i = (q % 2) * 3 + k
            out_ref[k * 4 + q] = jnp.where(c == q // 2, keep_ref[i], recv_ref[i])
        out_ref[IDLE * 4 + q] = note


def pack(ctl, keep, recv, sums):
    return pl.pallas_call(
        pack_kernel,
        in_specs=[SMEM, VMEM, VMEM, VMEM],
        out_specs=VMEM,
        out_shape=jax.ShapeDtypeStruct((16, SHARD, HALF), BF16),
        compiler_params=params(16),
    )(ctl, keep, recv, sums)


def fill(ref, scratch):
    pad = jnp.zeros((ROWS - SHARD, HALF), F32)
    for i in range(16):
        block = jnp.concatenate([ref[i].astype(F32), pad], axis=0)
        scratch[i * ROWS : (i + 1) * ROWS] = block.astype(BF16)


def index_grid(shape):
    return lax.broadcasted_iota(jnp.int32, shape, 0), lax.broadcasted_iota(jnp.int32, shape, 1)


def split(value):
    high = value.astype(BF16).astype(F32)
    return jnp.concatenate([high, value - high], axis=1)


def gram_kernel(c_ref, own_ref, oth_ref, p0_ref, p1_ref, p2_ref, p3_ref, xs, ys, out_ref):
    first = c_ref[0] == 0
    fill(own_ref, xs)
    fill(oth_ref, ys)
    row, col = index_grid((BLK, BLK))
    x0, x1 = xs[:, :BLK], xs[:, BLK:]
    y0, y1 = ys[:, :BLK], ys[:, BLK:]
    g00, g11 = dot_rows(x0, x0), dot_rows(x1, x1)
    diag1 = jnp.sum(jnp.where(row == col, g11, 0.0), axis=0, keepdims=True)
    out_ref[0:BLK] = jnp.where(row <= col, g00, g11).astype(BF16)
    out_ref[BLK : 2 * BLK] = dot_rows(x0, x1).astype(BF16)
    out_ref[2 * BLK : 3 * BLK] = dot_rows(x0, jnp.where(first, y0, y1)).astype(BF16)
    out_ref[3 * BLK : 4 * BLK] = dot_rows(x1, jnp.where(first, y1, y0)).astype(BF16)
    out_ref[4 * BLK :] = jnp.broadcast_to(diag1, (4 * CHUNK - 4 * BLK, BLK)).astype(BF16)
    note = xs[0:16, :BLK].astype(F32)
    for i in range(1, 16):
        note = note + xs[i * ROWS : i * ROWS + 16, :BLK].astype(F32)
    note = split(note[:, :128] + note[:, 128:])
    idle = c_ref[1] == 1
    for j, ref in enumerate((p0_ref, p1_ref, p2_ref, p3_ref)):
        start = pl.multiple_of(lax.rem(c_ref[2] + j, 4) * CHUNK, 16)
        ref[...] = out_ref[pl.ds(start, CHUNK)]
        ref[:16] = jnp.where(idle, note, ref[:16].astype(F32)).astype(BF16)


def partial_gram(ctl, own, oth):
    return pl.pallas_call(
        gram_kernel,
        in_specs=[SMEM, VMEM, VMEM],
        out_specs=[VMEM] * 4,
        out_shape=[jax.ShapeDtypeStruct((CHUNK, BLK), BF16)] * 4,
        scratch_shapes=[pltpu.VMEM((16 * ROWS, HALF), BF16)] * 2
        + [pltpu.VMEM((4 * CHUNK, BLK), BF16)],
        compiler_params=params(32),
    )(ctl, own, oth)


def sum_kernel(c_ref, p0_ref, p1_ref, p2_ref, p3_ref, out_ref):
    total = p0_ref[...].astype(F32) + p1_ref[...].astype(F32)
    total = total + (p2_ref[...].astype(F32) + p3_ref[...].astype(F32))
    out_ref[...] = total.astype(BF16)
    row, _ = index_grid((16, BLK))
    note = p0_ref[:16].astype(F32)
    for j, ref in enumerate((p1_ref, p2_ref, p3_ref)):
        note = jnp.where(row >= 4 * j + 4, ref[:16].astype(F32), note)
    out_ref[:16] = jnp.where(c_ref[1] == 1, note, total[:16]).astype(BF16)


def sum_parts(ctl, parts):
    return pl.pallas_call(
        sum_kernel,
        in_specs=[SMEM] + [VMEM] * 4,
        out_specs=VMEM,
        out_shape=jax.ShapeDtypeStruct((CHUNK, BLK), BF16),
        compiler_params=params(16),
    )(ctl, *parts)


def unpack(ref):
    blocks, at = [], 0
    for _ in range(4):
        pieces, need = [], BLK
        while need:
            chunk, offset = divmod(at, CHUNK)
            take = min(need, CHUNK - offset)
            pieces.append(ref[chunk, offset : offset + take])
            at, need = at + take, need - take
        piece = pieces[0] if len(pieces) == 1 else jnp.concatenate(pieces, axis=0)
        blocks.append(piece.astype(F32))
    offset = at - 3 * CHUNK
    return blocks, ref[3, offset : offset + 16].astype(F32)[0:1]


def polynomial_kernel(
    c_ref, own_ref, oth_ref, xo_ref, xt_ref, out_ref, xs, ys, a32, ab, m32, mb, c32, cb, gb, w32, nb, wb
):
    first = c_ref[0] == 0
    idle = c_ref[1] == 1
    fill(xo_ref, xs)
    fill(xt_ref, ys)
    row, col = index_grid((BLK, BLK))
    (d_o, o01, p2, p3), e_o = unpack(own_ref)
    (d_t, t01, r2, r3), e_t = unpack(oth_ref)

    trace = jnp.sum(jnp.where(row == col, d_o + d_t, 0.0), axis=0, keepdims=True) + (e_o + e_t)
    scale = lax.rsqrt(jnp.sum(trace, axis=1, keepdims=True))
    square = scale * scale

    def put(i, j, value):
        value = value * square
        a32[i * BLK : (i + 1) * BLK, j * BLK : (j + 1) * BLK] = value
        ab[i * BLK : (i + 1) * BLK, j * BLK : (j + 1) * BLK] = value.astype(BF16)

    def put_pair(i, j, value, turned):
        put(i, j, value)
        put(j, i, turned)

    for base, packed, edge, off in ((0, d_o, e_o, o01), (2, d_t, e_t, t01)):
        turned = packed.T
        put(base, base, jnp.where(row <= col, packed, turned))
        upper = jnp.where(row == col, jnp.broadcast_to(edge, (BLK, BLK)), turned)
        put(base + 1, base + 1, jnp.where(row > col, packed, upper))
        put_pair(base, base + 1, off, off.T)
    p2t, p3t, r2t, r3t = p2.T, p3.T, r2.T, r3.T
    put_pair(0, 2, jnp.where(first, p2, r2t), jnp.where(first, p2t, r2))
    put_pair(0, 3, jnp.where(first, r3t, p2), jnp.where(first, r3, p2t))
    put_pair(1, 2, jnp.where(first, r2t, p3), jnp.where(first, r2, p3t))
    put_pair(1, 3, jnp.where(first, p3, r3t), jnp.where(first, p3t, r3))

    blocks = [slice(i * BLK, (i + 1) * BLK) for i in range(4)]
    def mirrored(i, value, half, full):
        for j in range(i, 4):
            block = value[:, (j - i) * BLK : (j - i + 1) * BLK]
            pairs = ((i, j, block),) if i == j else ((i, j, block), (j, i, block.T))
            for r, c, piece in pairs:
                full[blocks[r], blocks[c]] = piece.astype(BF16)
                if half is not None and c < 2:
                    half[blocks[r], blocks[c]] = piece

    for i, s in enumerate(blocks):
        right = slice(i * BLK, FF)
        mirrored(i, COEF_Q * a32[s, right] + COEF_T * dot(ab[s], ab[:, right]), m32, mb)
    for i, s in enumerate(blocks):
        right = slice(i * BLK, FF)
        prod = COEF_P * a32[s, right] + dot(ab[s], mb[:, right])
        c32[s, right] = prod
        mirrored(i, prod, None, cb)
    for i, s in enumerate(blocks):
        right = slice(i * BLK, FF)
        mirrored(i, COEF_P * c32[s, right] + dot(cb[s], mb[:, right]), a32, gb)
    for s in blocks:
        poly = COEF_Q * a32[s, :HALF] + COEF_T * dot(gb[s], gb[:, :HALF])
        nb[s] = poly.astype(BF16)
        w32[s] = COEF_P * (poly + m32[s])
    for s in blocks:
        wb[s] = (w32[s] + dot(mb[s], nb[...])).astype(BF16)

    norms = own_ref[0, :16].astype(F32) + oth_ref[0, :16].astype(F32)
    for i in range(1, 4):
        norms = norms + (own_ref[i, :16].astype(F32) + oth_ref[i, :16].astype(F32))
    norms = norms[:, :128] + norms[:, 128:]
    note = jnp.concatenate([norms[4 * j : 4 * j + 1] for j in range(4)], axis=1)
    high = note.astype(BF16).astype(F32)
    spot = lax.broadcasted_iota(jnp.int32, (ROWS, HALF), 0)
    note = jnp.where(spot < 16, high, note - high)
    factor = scale * math.sqrt(D)
    for s in blocks:
        own = xs[s]
        value = dot(own, wb[:HALF]) + dot(ys[s], wb[HALF:])
        value = (value + (COEF_P * COEF_P) * own.astype(F32)) * factor
        for i in range(BLK // ROWS):
            piece = jnp.where(idle, note, value[i * ROWS : (i + 1) * ROWS])
            out_ref[s.start // ROWS + i] = piece[:SHARD].astype(BF16)


def polynomial(core, own_gram, oth_gram, own, oth):
    square = (FF, FF)
    tall = (FF, HALF)
    return pl.pallas_call(
        polynomial_kernel,
        in_specs=[SMEM, VMEM, VMEM, VMEM, VMEM],
        out_specs=VMEM,
        out_shape=jax.ShapeDtypeStruct((16, SHARD, HALF), BF16),
        scratch_shapes=[
            pltpu.VMEM((16 * ROWS, HALF), BF16),
            pltpu.VMEM((16 * ROWS, HALF), BF16),
            pltpu.VMEM(square, F32),
            pltpu.VMEM(square, BF16),
            pltpu.VMEM(tall, F32),
            pltpu.VMEM(square, BF16),
            pltpu.VMEM(square, F32),
            pltpu.VMEM(square, BF16),
            pltpu.VMEM(square, BF16),
            pltpu.VMEM(tall, F32),
            pltpu.VMEM(tall, BF16),
            pltpu.VMEM(tall, BF16),
        ],
        compiler_params=params(48),
    )(core, own_gram, oth_gram, own, oth)


def join_kernel(c_ref, own_ref, oth_ref, out_ref):
    c = c_ref[0]
    for i in range(6):
        slot = (i % 3) * 4 + 2 * c + i // 3
        own, oth = own_ref[slot], oth_ref[slot]
        out_ref[i, :, :HALF] = jnp.where(c == 0, own, oth)
        out_ref[i, :, HALF:] = jnp.where(c == 0, oth, own)


def join(ctl, own, oth):
    return pl.pallas_call(
        join_kernel,
        in_specs=[SMEM, VMEM, VMEM],
        out_specs=VMEM,
        out_shape=jax.ShapeDtypeStruct((6, SHARD, FF), BF16),
        compiler_params=params(16),
    )(ctl, own, oth)


def swap(value):
    return lax.ppermute(value, "c", [(0, 1), (1, 0)])


def owner_rms(note, owners):
    norms = note[0].astype(F32) + note[16].astype(F32)
    norms = norms.reshape(4, 128)[:, :12].reshape(4, 4, 3)
    x = lax.axis_index("x")
    table = owners.reshape(4, 4, 3)
    turned = jnp.stack([lax.dynamic_index_in_dim(table, (x - j) % 4, 0, False) for j in range(4)])
    me = (lax.axis_index("a") * 4 + lax.axis_index("b")) * 4 + lax.axis_index("y")
    return jnp.sqrt(jnp.sum(jnp.where(turned == me, norms, 0.0)) / (D * FF)).reshape(1)


def between(value, shift):
    pairs = []
    for a, b, y, x in itertools.product(range(4), repeat=4):
        target = (a, b, y, (x + shift) % 4) if b == IDLE else ((a + shift) % 4, b, y, x)
        pairs.append(tuple(((h * 4 + i) * 4 + j) * 4 + k for h, i, j, k in ((a, b, y, x), target)))
    return lax.ppermute(value, ("a", "b", "y", "x"), pairs)


def shards(grad, momentum, owners):
    shape = grad.shape
    core, a, b = (lax.axis_index(name).astype(jnp.int32) for name in ("c", "a", "b"))
    ctl = jnp.stack([core, (b == IDLE).astype(jnp.int32), a])
    flat = (6, SHARD, FF)
    grad = pltpu.with_memory_space_constraint(grad.reshape(flat), pltpu.HBM)
    momentum = pltpu.with_memory_space_constraint(momentum.reshape(flat), pltpu.HBM)
    keep, send, sums = blend(ctl, grad, momentum)
    packed = pack(ctl, keep, swap(send), sums)
    own = lax.all_to_all(packed, ("b", "y"), 0, 0, tiled=True)
    oth = swap(own)
    partial = partial_gram(ctl, own, oth)
    parts = [partial[0]] + [between(partial[j], j) for j in (1, 2, 3)]
    momentum_new = new_momentum(grad, momentum, partial[0])
    *parts, momentum_new = lax.optimization_barrier((*parts, momentum_new))
    own_gram = lax.all_gather(sum_parts(ctl, parts), "a", axis=0)
    oth_gram = swap(own_gram)
    finished = polynomial(ctl, own_gram, oth_gram, own, oth)
    back = lax.all_to_all(finished, ("b", "y"), 0, 0, tiled=True)
    update = join(ctl, back, swap(back))
    owned_rms = owner_rms(back[IDLE * 4], owners)
    return (momentum_new.reshape(shape), update.reshape(shape), owned_rms)


def solution(mesh):
    fine = Mesh(mesh.devices.reshape(4, 4, 4, 4, 2), ("a", "b", "y", "x", "c"))
    rows = ("a", "b", "y")
    wide = P(("x", "c"), None, rows, None)
    return jax.shard_map(
        shards, mesh=fine, in_specs=(wide, wide, P()), out_specs=(wide, wide, P(rows)), check_vma=False
    )
```

```python
import itertools
import math

import jax
import jax.numpy as jnp
from jax import lax
from jax.experimental import pallas as pl
from jax.experimental.pallas import tpu as pltpu
from jax.sharding import Mesh
from jax.sharding import PartitionSpec as P

D = 3584
FF = 1024
HALF = FF // 2
BLK = 256
SHARD = 56
ROWS = 64
CHUNK = 272

MU = 0.95
COEF_P = 3.4445
COEF_Q = -4.775
COEF_T = 2.0315

IDLE = 3


F32 = jnp.float32
BF16 = jnp.bfloat16
VMEM = pl.BlockSpec(memory_space=pltpu.VMEM)
SMEM = pl.BlockSpec(memory_space=pltpu.SMEM)


def params(mib):
    return pltpu.CompilerParams(vmem_limit_bytes=mib * 1024 * 1024)


def dot(a, b):
    return jnp.dot(a, b, preferred_element_type=F32)


def dot_rows(a, b):
    return lax.dot_general(a, b, (((0,), (0,)), ((), ())), preferred_element_type=F32)


def loads(grad_ref, mom_ref, gbuf, mbuf, gsem, msem):
    copies = []
    for i in range(gbuf.shape[0]):
        copies.append(
            (
                pltpu.make_async_copy(grad_ref.at[i], gbuf.at[i], gsem.at[i]),
                pltpu.make_async_copy(mom_ref.at[i], mbuf.at[i], msem.at[i]),
            )
        )
    for pair in copies:
        for copy in pair:
            copy.start()
    return copies


def blend_kernel(c_ref, grad_ref, mom_ref, keep_ref, send_ref, sum_ref, gbuf, mbuf, gsem, msem):
    first = c_ref[0] == 0
    for i, pair in enumerate(loads(grad_ref, mom_ref, gbuf, mbuf, gsem, msem)):
        for copy in pair:
            copy.wait()
        grad = gbuf[i]
        blended = (grad + MU * (MU * mbuf[i] + grad)).astype(BF16)
        left, right = blended[:, :HALF], blended[:, HALF:]
        keep_ref[i] = jnp.where(first, left, right)
        send_ref[i] = jnp.where(first, right, left)
        rounded = blended.astype(F32)
        total = jnp.sum(jnp.sum(rounded * rounded, axis=0, keepdims=True), axis=1, keepdims=True)
        sum_ref[i] = jnp.broadcast_to(total, (8, 128))


def momentum_kernel(grad_ref, mom_ref, after_ref, new_ref, gbuf, mbuf, gsem, msem, nsem):
    stores = []
    for i, pair in enumerate(loads(grad_ref, mom_ref, gbuf, mbuf, gsem, msem)):
        for copy in pair:
            copy.wait()
        mbuf[i] = MU * mbuf[i] + gbuf[i]
        store = pltpu.make_async_copy(mbuf.at[i], new_ref.at[i], nsem.at[i])
        store.start()
        stores.append(store)
    for store in stores:
        store.wait()


def buffers(count, groups):
    whole = pltpu.VMEM((count, SHARD, FF), F32)
    return [whole, whole] + [pltpu.SemaphoreType.DMA((count,))] * groups


HBM = pl.BlockSpec(memory_space=pltpu.HBM)


def blend(ctl, grad, momentum):
    count = grad.shape[0]
    return pl.pallas_call(
        blend_kernel,
        in_specs=[SMEM, HBM, HBM],
        out_specs=[VMEM, VMEM, VMEM],
        out_shape=[
            jax.ShapeDtypeStruct((count, SHARD, HALF), BF16),
            jax.ShapeDtypeStruct((count, SHARD, HALF), BF16),
            jax.ShapeDtypeStruct((count, 8, 128), F32),
        ],
        scratch_shapes=buffers(count, 2),
        compiler_params=params(24),
    )(ctl, grad, momentum)


def new_momentum(grad, momentum, after):
    return pl.pallas_call(
        momentum_kernel,
        in_specs=[HBM, HBM, pl.BlockSpec(memory_space=pl.ANY)],
        out_specs=HBM,
        out_shape=jax.ShapeDtypeStruct(grad.shape, F32),
        scratch_shapes=buffers(grad.shape[0], 3),
        compiler_params=params(24),
    )(grad, momentum, after)


def pack_kernel(c_ref, keep_ref, recv_ref, sum_ref, out_ref):
    c = c_ref[0]
    lane = lax.broadcasted_iota(jnp.int32, (8, 128), 1)
    sums = jnp.zeros((8, 128), F32)
    for k in range(3):
        for g in range(2):
            sums = jnp.where(lane == (2 * c + g) * 3 + k, sum_ref[g * 3 + k], sums)
    high = sums.astype(BF16).astype(F32)
    note = jnp.concatenate([high, sums - high, jnp.zeros((8, HALF - 256), F32)], axis=1)
    note = jnp.concatenate([note] * (SHARD // 8), axis=0).astype(BF16)
    for q in range(4):
        for k in range(3):
            i = (q % 2) * 3 + k
            out_ref[k * 4 + q] = jnp.where(c == q // 2, keep_ref[i], recv_ref[i])
        out_ref[IDLE * 4 + q] = note


def pack(ctl, keep, recv, sums):
    return pl.pallas_call(
        pack_kernel,
        in_specs=[SMEM, VMEM, VMEM, VMEM],
        out_specs=VMEM,
        out_shape=jax.ShapeDtypeStruct((16, SHARD, HALF), BF16),
        compiler_params=params(16),
    )(ctl, keep, recv, sums)


def fill(ref, scratch):
    pad = jnp.zeros((ROWS - SHARD, HALF), F32)
    for i in range(16):
        block = jnp.concatenate([ref[i].astype(F32), pad], axis=0)
        scratch[i * ROWS : (i + 1) * ROWS] = block.astype(BF16)


def index_grid(shape):
    return lax.broadcasted_iota(jnp.int32, shape, 0), lax.broadcasted_iota(jnp.int32, shape, 1)


def split(value):
    high = value.astype(BF16).astype(F32)
    return jnp.concatenate([high, value - high], axis=1)


def gram_kernel(c_ref, own_ref, oth_ref, p0_ref, p1_ref, p2_ref, p3_ref, xs, ys, out_ref):
    first = c_ref[0] == 0
    fill(own_ref, xs)
    fill(oth_ref, ys)
    row, col = index_grid((BLK, BLK))
    x0, x1 = xs[:, :BLK], xs[:, BLK:]
    y0, y1 = ys[:, :BLK], ys[:, BLK:]
    g00, g11 = dot_rows(x0, x0), dot_rows(x1, x1)
    diag1 = jnp.sum(jnp.where(row == col, g11, 0.0), axis=0, keepdims=True)
    out_ref[0:BLK] = jnp.where(row <= col, g00, g11).astype(BF16)
    out_ref[BLK : 2 * BLK] = dot_rows(x0, x1).astype(BF16)
    out_ref[2 * BLK : 3 * BLK] = dot_rows(x0, jnp.where(first, y0, y1)).astype(BF16)
    out_ref[3 * BLK : 4 * BLK] = dot_rows(x1, jnp.where(first, y1, y0)).astype(BF16)
    out_ref[4 * BLK :] = jnp.broadcast_to(diag1, (4 * CHUNK - 4 * BLK, BLK)).astype(BF16)
    note = xs[0:16, :BLK].astype(F32)
    for i in range(1, 16):
        note = note + xs[i * ROWS : i * ROWS + 16, :BLK].astype(F32)
    note = split(note[:, :128] + note[:, 128:])
    idle = c_ref[1] == 1
    for j, ref in enumerate((p0_ref, p1_ref, p2_ref, p3_ref)):
        start = pl.multiple_of(lax.rem(c_ref[2] + j, 4) * CHUNK, 16)
        ref[...] = out_ref[pl.ds(start, CHUNK)]
        ref[:16] = jnp.where(idle, note, ref[:16].astype(F32)).astype(BF16)


def partial_gram(ctl, own, oth):
    return pl.pallas_call(
        gram_kernel,
        in_specs=[SMEM, VMEM, VMEM],
        out_specs=[VMEM] * 4,
        out_shape=[jax.ShapeDtypeStruct((CHUNK, BLK), BF16)] * 4,
        scratch_shapes=[pltpu.VMEM((16 * ROWS, HALF), BF16)] * 2
        + [pltpu.VMEM((4 * CHUNK, BLK), BF16)],
        compiler_params=params(32),
    )(ctl, own, oth)


def sum_kernel(c_ref, p0_ref, p1_ref, p2_ref, p3_ref, out_ref):
    total = p0_ref[...].astype(F32) + p1_ref[...].astype(F32)
    total = total + (p2_ref[...].astype(F32) + p3_ref[...].astype(F32))
    out_ref[...] = total.astype(BF16)
    note = p0_ref[:16].astype(F32)
    for j, ref in enumerate((p1_ref, p2_ref, p3_ref)):
        note = jnp.where(c_ref[3] == j + 1, ref[:16].astype(F32), note)
    out_ref[:16] = jnp.where(c_ref[1] == 1, note, total[:16]).astype(BF16)


def sum_parts(ctl, parts):
    return pl.pallas_call(
        sum_kernel,
        in_specs=[SMEM] + [VMEM] * 4,
        out_specs=VMEM,
        out_shape=jax.ShapeDtypeStruct((CHUNK, BLK), BF16),
        compiler_params=params(16),
    )(ctl, *parts)


def unpack(ref):
    blocks, at = [], 0
    for _ in range(4):
        pieces, need = [], BLK
        while need:
            chunk, offset = divmod(at, CHUNK)
            take = min(need, CHUNK - offset)
            pieces.append(ref[chunk, offset : offset + take])
            at, need = at + take, need - take
        piece = pieces[0] if len(pieces) == 1 else jnp.concatenate(pieces, axis=0)
        blocks.append(piece.astype(F32))
    offset = at - 3 * CHUNK
    return blocks, ref[3, offset : offset + 16].astype(F32)[0:1]


def polynomial_kernel(
    c_ref, own_ref, oth_ref, xo_ref, xt_ref, out_ref, xs, ys, a32, ab, m32, mb, c32, cb, gb, w32, nb, wb
):
    first = c_ref[0] == 0
    idle = c_ref[1] == 1
    fill(xo_ref, xs)
    fill(xt_ref, ys)
    row, col = index_grid((BLK, BLK))
    (d_o, o01, p2, p3), e_o = unpack(own_ref)
    (d_t, t01, r2, r3), e_t = unpack(oth_ref)

    trace = jnp.sum(jnp.where(row == col, d_o + d_t, 0.0), axis=0, keepdims=True) + (e_o + e_t)
    scale = lax.rsqrt(jnp.sum(trace, axis=1, keepdims=True))
    square = scale * scale

    def put(i, j, value):
        value = value * square
        a32[i * BLK : (i + 1) * BLK, j * BLK : (j + 1) * BLK] = value
        ab[i * BLK : (i + 1) * BLK, j * BLK : (j + 1) * BLK] = value.astype(BF16)

    def put_pair(i, j, value, turned):
        put(i, j, value)
        put(j, i, turned)

    for base, packed, edge, off in ((0, d_o, e_o, o01), (2, d_t, e_t, t01)):
        turned = packed.T
        put(base, base, jnp.where(row <= col, packed, turned))
        upper = jnp.where(row == col, jnp.broadcast_to(edge, (BLK, BLK)), turned)
        put(base + 1, base + 1, jnp.where(row > col, packed, upper))
        put_pair(base, base + 1, off, off.T)
    p2t, p3t, r2t, r3t = p2.T, p3.T, r2.T, r3.T
    put_pair(0, 2, jnp.where(first, p2, r2t), jnp.where(first, p2t, r2))
    put_pair(0, 3, jnp.where(first, r3t, p2), jnp.where(first, r3, p2t))
    put_pair(1, 2, jnp.where(first, r2t, p3), jnp.where(first, r2, p3t))
    put_pair(1, 3, jnp.where(first, p3, r3t), jnp.where(first, p3t, r3))

    blocks = [slice(i * BLK, (i + 1) * BLK) for i in range(4)]
    def mirrored(i, value, half, full):
        for j in range(i, 4):
            block = value[:, (j - i) * BLK : (j - i + 1) * BLK]
            pairs = ((i, j, block),) if i == j else ((i, j, block), (j, i, block.T))
            for r, c, piece in pairs:
                full[blocks[r], blocks[c]] = piece.astype(BF16)
                if half is not None and c < 2:
                    half[blocks[r], blocks[c]] = piece

    for i, s in enumerate(blocks):
        right = slice(i * BLK, FF)
        mirrored(i, COEF_Q * a32[s, right] + COEF_T * dot(ab[s], ab[:, right]), m32, mb)
    for i, s in enumerate(blocks):
        right = slice(i * BLK, FF)
        prod = COEF_P * a32[s, right] + dot(ab[s], mb[:, right])
        c32[s, right] = prod
        mirrored(i, prod, None, cb)
    for i, s in enumerate(blocks):
        right = slice(i * BLK, FF)
        mirrored(i, COEF_P * c32[s, right] + dot(cb[s], mb[:, right]), a32, gb)
    for s in blocks:
        poly = COEF_Q * a32[s, :HALF] + COEF_T * dot(gb[s], gb[:, :HALF])
        nb[s] = poly.astype(BF16)
        w32[s] = COEF_P * (poly + m32[s])
    for s in blocks:
        wb[s] = (w32[s] + dot(mb[s], nb[...])).astype(BF16)

    notes = [own_ref[i, :16].astype(F32) + oth_ref[i, :16].astype(F32) for i in range(4)]
    note = jnp.concatenate([(n[:, :128] + n[:, 128:])[0:1] for n in notes], axis=1)
    high = note.astype(BF16).astype(F32)
    spot = lax.broadcasted_iota(jnp.int32, (ROWS, HALF), 0)
    note = jnp.where(spot < 16, high, note - high)
    factor = scale * math.sqrt(D)
    for s in blocks:
        own = xs[s]
        value = dot(own, wb[:HALF]) + dot(ys[s], wb[HALF:])
        value = (value + (COEF_P * COEF_P) * own.astype(F32)) * factor
        for i in range(BLK // ROWS):
            piece = jnp.where(idle, note, value[i * ROWS : (i + 1) * ROWS])
            out_ref[s.start // ROWS + i] = piece[:SHARD].astype(BF16)


def polynomial(core, own_gram, oth_gram, own, oth):
    square = (FF, FF)
    tall = (FF, HALF)
    return pl.pallas_call(
        polynomial_kernel,
        in_specs=[SMEM, VMEM, VMEM, VMEM, VMEM],
        out_specs=VMEM,
        out_shape=jax.ShapeDtypeStruct((16, SHARD, HALF), BF16),
        scratch_shapes=[
            pltpu.VMEM((16 * ROWS, HALF), BF16),
            pltpu.VMEM((16 * ROWS, HALF), BF16),
            pltpu.VMEM(square, F32),
            pltpu.VMEM(square, BF16),
            pltpu.VMEM(tall, F32),
            pltpu.VMEM(square, BF16),
            pltpu.VMEM(square, F32),
            pltpu.VMEM(square, BF16),
            pltpu.VMEM(square, BF16),
            pltpu.VMEM(tall, F32),
            pltpu.VMEM(tall, BF16),
            pltpu.VMEM(tall, BF16),
        ],
        compiler_params=params(48),
    )(core, own_gram, oth_gram, own, oth)


def join_kernel(c_ref, own_ref, oth_ref, out_ref):
    c = c_ref[0]
    for i in range(6):
        slot = (i % 3) * 4 + 2 * c + i // 3
        own, oth = own_ref[slot], oth_ref[slot]
        out_ref[i, :, :HALF] = jnp.where(c == 0, own, oth)
        out_ref[i, :, HALF:] = jnp.where(c == 0, oth, own)


def join(ctl, own, oth):
    return pl.pallas_call(
        join_kernel,
        in_specs=[SMEM, VMEM, VMEM],
        out_specs=VMEM,
        out_shape=jax.ShapeDtypeStruct((6, SHARD, FF), BF16),
        compiler_params=params(16),
    )(ctl, own, oth)


def swap(value):
    return lax.ppermute(value, "c", [(0, 1), (1, 0)])


def owner_rms(notes, owners):
    norms = jnp.sum(notes[:, 0].astype(F32) + notes[:, 16].astype(F32), axis=0)
    norms = norms.reshape(4, 128)[:, :12].reshape(owners.shape)
    me = (lax.axis_index("a") * 4 + lax.axis_index("b")) * 4 + lax.axis_index("y")
    return jnp.sqrt(jnp.sum(jnp.where(owners == me, norms, 0.0)) / (D * FF)).reshape(1)


def between(value, shift):
    pairs = []
    for a, b, y, x in itertools.product(range(4), repeat=4):
        if b != IDLE or y == shift:
            ends = ((a, b, y, x), ((a + shift) % 4, b, y, x))
            pairs.append(tuple(((h * 4 + i) * 4 + j) * 4 + k for h, i, j, k in ends))
    return lax.ppermute(value, ("a", "b", "y", "x"), pairs)


def gather(value):
    groups = [[(a * 4 + b) * 4 + x for a in range(4)] for b in range(IDLE) for x in range(4)]
    groups += [[(a * 4 + IDLE) * 4 + x for x in range(4)] for a in range(4)]
    return lax.all_gather(value, ("a", "b", "x"), axis=0, axis_index_groups=groups)


def shards(grad, momentum, owners):
    shape = grad.shape
    core, a, b = (lax.axis_index(name).astype(jnp.int32) for name in ("c", "a", "b"))
    y = lax.axis_index("y").astype(jnp.int32)
    ctl = jnp.stack([core, (b == IDLE).astype(jnp.int32), a, y])
    flat = (6, SHARD, FF)
    grad = pltpu.with_memory_space_constraint(grad.reshape(flat), pltpu.HBM)
    momentum = pltpu.with_memory_space_constraint(momentum.reshape(flat), pltpu.HBM)
    keep, send, sums = blend(ctl, grad, momentum)
    packed = pack(ctl, keep, swap(send), sums)
    own = lax.all_to_all(packed, ("b", "y"), 0, 0, tiled=True)
    oth = swap(own)
    partial = partial_gram(ctl, own, oth)
    parts = [partial[0]] + [between(partial[j], j) for j in (1, 2, 3)]
    momentum_new = new_momentum(grad, momentum, partial[0])
    *parts, momentum_new = lax.optimization_barrier((*parts, momentum_new))
    own_gram = gather(sum_parts(ctl, parts))
    oth_gram = swap(own_gram)
    finished = polynomial(ctl, own_gram, oth_gram, own, oth)
    back = lax.all_to_all(finished, ("b", "y"), 0, 0, tiled=True)
    update = join(ctl, back, swap(back))
    owned_rms = owner_rms(back[IDLE * 4 :], owners)
    return (momentum_new.reshape(shape), update.reshape(shape), owned_rms)


def solution(mesh):
    fine = Mesh(mesh.devices.reshape(4, 4, 4, 4, 2), ("a", "b", "y", "x", "c"))
    rows = ("a", "b", "y")
    wide = P(("x", "c"), None, rows, None)
    return jax.shard_map(
        shards, mesh=fine, in_specs=(wide, wide, P()), out_specs=(wide, wide, P(rows)), check_vma=False
    )
```

```python
import itertools
import math

import jax
import jax.numpy as jnp
from jax import lax
from jax.experimental import pallas as pl
from jax.experimental.pallas import tpu as pltpu
from jax.sharding import Mesh
from jax.sharding import PartitionSpec as P

D = 3584
FF = 1024
HALF = FF // 2
BLK = 256
SHARD = 56
ROWS = 64
CHUNK = 272

MU = 0.95
COEF_P = 3.4445
COEF_Q = -4.775
COEF_T = 2.0315

IDLE = 3


F32 = jnp.float32
BF16 = jnp.bfloat16
VMEM = pl.BlockSpec(memory_space=pltpu.VMEM)
SMEM = pl.BlockSpec(memory_space=pltpu.SMEM)


def params(mib):
    return pltpu.CompilerParams(vmem_limit_bytes=mib * 1024 * 1024)


def dot(a, b):
    return jnp.dot(a, b, preferred_element_type=F32)


def dot_rows(a, b):
    return lax.dot_general(a, b, (((0,), (0,)), ((), ())), preferred_element_type=F32)


def loads(grad_ref, mom_ref, gbuf, mbuf, gsem, msem):
    copies = []
    for i in range(gbuf.shape[0]):
        copies.append(
            (
                pltpu.make_async_copy(grad_ref.at[i], gbuf.at[i], gsem.at[i]),
                pltpu.make_async_copy(mom_ref.at[i], mbuf.at[i], msem.at[i]),
            )
        )
    for pair in copies:
        for copy in pair:
            copy.start()
    return copies


def blend_kernel(c_ref, grad_ref, mom_ref, keep_ref, send_ref, sum_ref, gbuf, mbuf, gsem, msem):
    first = c_ref[0] == 0
    for i, pair in enumerate(loads(grad_ref, mom_ref, gbuf, mbuf, gsem, msem)):
        for copy in pair:
            copy.wait()
        grad = gbuf[i]
        blended = (grad + MU * (MU * mbuf[i] + grad)).astype(BF16)
        left, right = blended[:, :HALF], blended[:, HALF:]
        keep_ref[i] = jnp.where(first, left, right)
        send_ref[i] = jnp.where(first, right, left)
        rounded = blended.astype(F32)
        total = jnp.sum(jnp.sum(rounded * rounded, axis=0, keepdims=True), axis=1, keepdims=True)
        sum_ref[i] = jnp.broadcast_to(total, (8, 128))


def momentum_kernel(grad_ref, mom_ref, after_ref, new_ref, gbuf, mbuf, gsem, msem, nsem):
    stores = []
    for i, pair in enumerate(loads(grad_ref, mom_ref, gbuf, mbuf, gsem, msem)):
        for copy in pair:
            copy.wait()
        mbuf[i] = MU * mbuf[i] + gbuf[i]
        store = pltpu.make_async_copy(mbuf.at[i], new_ref.at[i], nsem.at[i])
        store.start()
        stores.append(store)
    for store in stores:
        store.wait()


def buffers(count, groups):
    whole = pltpu.VMEM((count, SHARD, FF), F32)
    return [whole, whole] + [pltpu.SemaphoreType.DMA((count,))] * groups


HBM = pl.BlockSpec(memory_space=pltpu.HBM)


def blend(ctl, grad, momentum):
    count = grad.shape[0]
    return pl.pallas_call(
        blend_kernel,
        in_specs=[SMEM, HBM, HBM],
        out_specs=[VMEM, VMEM, VMEM],
        out_shape=[
            jax.ShapeDtypeStruct((count, SHARD, HALF), BF16),
            jax.ShapeDtypeStruct((count, SHARD, HALF), BF16),
            jax.ShapeDtypeStruct((count, 8, 128), F32),
        ],
        scratch_shapes=buffers(count, 2),
        compiler_params=params(24),
    )(ctl, grad, momentum)


def new_momentum(grad, momentum, after):
    return pl.pallas_call(
        momentum_kernel,
        in_specs=[HBM, HBM, pl.BlockSpec(memory_space=pl.ANY)],
        out_specs=HBM,
        out_shape=jax.ShapeDtypeStruct(grad.shape, F32),
        scratch_shapes=buffers(grad.shape[0], 3),
        compiler_params=params(24),
    )(grad, momentum, after)


def pack_kernel(c_ref, keep_ref, recv_ref, sum_ref, out_ref):
    c = c_ref[0]
    lane = lax.broadcasted_iota(jnp.int32, (8, 128), 1)
    sums = jnp.zeros((8, 128), F32)
    for k in range(3):
        for g in range(2):
            sums = jnp.where(lane == (2 * c + g) * 3 + k, sum_ref[g * 3 + k], sums)
    high = sums.astype(BF16).astype(F32)
    note = jnp.concatenate([high, sums - high, jnp.zeros((8, HALF - 256), F32)], axis=1)
    note = jnp.concatenate([note] * (SHARD // 8), axis=0).astype(BF16)
    for q in range(4):
        for k in range(3):
            i = (q % 2) * 3 + k
            out_ref[k * 4 + q] = jnp.where(c == q // 2, keep_ref[i], recv_ref[i])
        out_ref[IDLE * 4 + q] = note


def pack(ctl, keep, recv, sums):
    return pl.pallas_call(
        pack_kernel,
        in_specs=[SMEM, VMEM, VMEM, VMEM],
        out_specs=VMEM,
        out_shape=jax.ShapeDtypeStruct((16, SHARD, HALF), BF16),
        compiler_params=params(16),
    )(ctl, keep, recv, sums)


def fill(ref, scratch):
    pad = jnp.zeros((ROWS - SHARD, HALF), F32)
    for i in range(16):
        block = jnp.concatenate([ref[i].astype(F32), pad], axis=0)
        scratch[i * ROWS : (i + 1) * ROWS] = block.astype(BF16)


def index_grid(shape):
    return lax.broadcasted_iota(jnp.int32, shape, 0), lax.broadcasted_iota(jnp.int32, shape, 1)


def split(value):
    high = value.astype(BF16).astype(F32)
    return jnp.concatenate([high, value - high], axis=1)


def gram_kernel(c_ref, own_ref, oth_ref, p0_ref, p1_ref, p2_ref, p3_ref, xs, ys, out_ref):
    first = c_ref[0] == 0
    fill(own_ref, xs)
    fill(oth_ref, ys)
    row, col = index_grid((BLK, BLK))
    x0, x1 = xs[:, :BLK], xs[:, BLK:]
    y0, y1 = ys[:, :BLK], ys[:, BLK:]
    g00, g11 = dot_rows(x0, x0), dot_rows(x1, x1)
    diag1 = jnp.sum(jnp.where(row == col, g11, 0.0), axis=0, keepdims=True)
    out_ref[0:BLK] = jnp.where(row <= col, g00, g11).astype(BF16)
    out_ref[BLK : 2 * BLK] = dot_rows(x0, x1).astype(BF16)
    out_ref[2 * BLK : 3 * BLK] = dot_rows(x0, jnp.where(first, y0, y1)).astype(BF16)
    out_ref[3 * BLK : 4 * BLK] = dot_rows(x1, jnp.where(first, y1, y0)).astype(BF16)
    out_ref[4 * BLK :] = jnp.broadcast_to(diag1, (4 * CHUNK - 4 * BLK, BLK)).astype(BF16)
    note = xs[0:16, :BLK].astype(F32)
    for i in range(1, 16):
        note = note + xs[i * ROWS : i * ROWS + 16, :BLK].astype(F32)
    note = split(note[:, :128] + note[:, 128:])
    idle = c_ref[1] == 1
    for j, ref in enumerate((p0_ref, p1_ref, p2_ref, p3_ref)):
        start = pl.multiple_of(lax.rem(c_ref[2] + j, 4) * CHUNK, 16)
        ref[...] = out_ref[pl.ds(start, CHUNK)]
        ref[:16] = jnp.where(idle, note, ref[:16].astype(F32)).astype(BF16)


def partial_gram(ctl, own, oth):
    return pl.pallas_call(
        gram_kernel,
        in_specs=[SMEM, VMEM, VMEM],
        out_specs=[VMEM] * 4,
        out_shape=[jax.ShapeDtypeStruct((CHUNK, BLK), BF16)] * 4,
        scratch_shapes=[pltpu.VMEM((16 * ROWS, HALF), BF16)] * 2
        + [pltpu.VMEM((4 * CHUNK, BLK), BF16)],
        compiler_params=params(32),
    )(ctl, own, oth)


def sum_kernel(c_ref, p0_ref, p1_ref, p2_ref, p3_ref, out_ref):
    total = p0_ref[...].astype(F32) + p1_ref[...].astype(F32)
    total = total + (p2_ref[...].astype(F32) + p3_ref[...].astype(F32))
    out_ref[...] = total.astype(BF16)
    note = p0_ref[:16].astype(F32)
    for j, ref in enumerate((p1_ref, p2_ref, p3_ref)):
        note = jnp.where(c_ref[3] == j + 1, ref[:16].astype(F32), note)
    out_ref[:16] = jnp.where(c_ref[1] == 1, note, total[:16]).astype(BF16)


def sum_parts(ctl, parts):
    return pl.pallas_call(
        sum_kernel,
        in_specs=[SMEM] + [VMEM] * 4,
        out_specs=VMEM,
        out_shape=jax.ShapeDtypeStruct((CHUNK, BLK), BF16),
        compiler_params=params(16),
    )(ctl, *parts)


def unpack(ref):
    blocks, at = [], 0
    for _ in range(4):
        pieces, need = [], BLK
        while need:
            chunk, offset = divmod(at, CHUNK)
            take = min(need, CHUNK - offset)
            pieces.append(ref[chunk, offset : offset + take])
            at, need = at + take, need - take
        piece = pieces[0] if len(pieces) == 1 else jnp.concatenate(pieces, axis=0)
        blocks.append(piece.astype(F32))
    offset = at - 3 * CHUNK
    return blocks, ref[3, offset : offset + 16].astype(F32)[0:1]


def polynomial_kernel(
    c_ref, own_ref, oth_ref, xo_ref, xt_ref, out_ref, xs, ys, a32, ab, m32, mb, c32, cb, gb, w32, nb, wb
):
    first = c_ref[0] == 0
    idle = c_ref[1] == 1
    fill(xo_ref, xs)
    fill(xt_ref, ys)
    row, col = index_grid((BLK, BLK))
    (d_o, o01, p2, p3), e_o = unpack(own_ref)
    (d_t, t01, r2, r3), e_t = unpack(oth_ref)

    trace = jnp.sum(jnp.where(row == col, d_o + d_t, 0.0), axis=0, keepdims=True) + (e_o + e_t)
    scale = lax.rsqrt(jnp.sum(trace, axis=1, keepdims=True))
    square = scale * scale

    def put(i, j, value):
        value = value * square
        a32[i * BLK : (i + 1) * BLK, j * BLK : (j + 1) * BLK] = value
        ab[i * BLK : (i + 1) * BLK, j * BLK : (j + 1) * BLK] = value.astype(BF16)

    def put_pair(i, j, value, turned):
        put(i, j, value)
        put(j, i, turned)

    for base, packed, edge, off in ((0, d_o, e_o, o01), (2, d_t, e_t, t01)):
        turned = packed.T
        put(base, base, jnp.where(row <= col, packed, turned))
        upper = jnp.where(row == col, jnp.broadcast_to(edge, (BLK, BLK)), turned)
        put(base + 1, base + 1, jnp.where(row > col, packed, upper))
        put_pair(base, base + 1, off, off.T)
    p2t, p3t, r2t, r3t = p2.T, p3.T, r2.T, r3.T
    put_pair(0, 2, jnp.where(first, p2, r2t), jnp.where(first, p2t, r2))
    put_pair(0, 3, jnp.where(first, r3t, p2), jnp.where(first, r3, p2t))
    put_pair(1, 2, jnp.where(first, r2t, p3), jnp.where(first, r2, p3t))
    put_pair(1, 3, jnp.where(first, p3, r3t), jnp.where(first, p3t, r3))

    blocks = [slice(i * BLK, (i + 1) * BLK) for i in range(4)]
    def mirrored(i, value, half, full):
        for j in range(i, 4):
            block = value[:, (j - i) * BLK : (j - i + 1) * BLK]
            pairs = ((i, j, block),) if i == j else ((i, j, block), (j, i, block.T))
            for r, c, piece in pairs:
                full[blocks[r], blocks[c]] = piece.astype(BF16)
                if half is not None and c < 2:
                    half[blocks[r], blocks[c]] = piece

    for i, s in enumerate(blocks):
        right = slice(i * BLK, FF)
        mirrored(i, COEF_Q * a32[s, right] + COEF_T * dot(ab[s], ab[:, right]), m32, mb)
    for i, s in enumerate(blocks):
        right = slice(i * BLK, FF)
        prod = COEF_P * a32[s, right] + dot(ab[s], mb[:, right])
        c32[s, right] = prod
        mirrored(i, prod, None, cb)
    for i, s in enumerate(blocks):
        right = slice(i * BLK, FF)
        mirrored(i, COEF_P * c32[s, right] + dot(cb[s], mb[:, right]), a32, gb)
    for s in blocks:
        poly = COEF_Q * a32[s, :HALF] + COEF_T * dot(gb[s], gb[:, :HALF])
        nb[s] = poly.astype(BF16)
        w32[s] = COEF_P * (poly + m32[s])
    for s in blocks:
        wb[s] = (w32[s] + dot(mb[s], nb[...])).astype(BF16)

    notes = [own_ref[i, :16].astype(F32) + oth_ref[i, :16].astype(F32) for i in range(4)]
    note = jnp.concatenate([(n[:, :128] + n[:, 128:])[0:1] for n in notes], axis=1)
    high = note.astype(BF16).astype(F32)
    spot = lax.broadcasted_iota(jnp.int32, (ROWS, HALF), 0)
    note = jnp.where(spot < 16, high, note - high)
    factor = scale * math.sqrt(D)
    for s in blocks:
        own = xs[s]
        value = dot(own, wb[:HALF]) + dot(ys[s], wb[HALF:])
        value = (value + (COEF_P * COEF_P) * own.astype(F32)) * factor
        for i in range(BLK // ROWS):
            piece = jnp.where(idle, note, value[i * ROWS : (i + 1) * ROWS])
            out_ref[s.start // ROWS + i] = piece[:SHARD].astype(BF16)


def polynomial(core, own_gram, oth_gram, own, oth):
    square = (FF, FF)
    tall = (FF, HALF)
    return pl.pallas_call(
        polynomial_kernel,
        in_specs=[SMEM, VMEM, VMEM, VMEM, VMEM],
        out_specs=VMEM,
        out_shape=jax.ShapeDtypeStruct((16, SHARD, HALF), BF16),
        scratch_shapes=[
            pltpu.VMEM((16 * ROWS, HALF), BF16),
            pltpu.VMEM((16 * ROWS, HALF), BF16),
            pltpu.VMEM(square, F32),
            pltpu.VMEM(square, BF16),
            pltpu.VMEM(tall, F32),
            pltpu.VMEM(square, BF16),
            pltpu.VMEM(square, F32),
            pltpu.VMEM(square, BF16),
            pltpu.VMEM(square, BF16),
            pltpu.VMEM(tall, F32),
            pltpu.VMEM(tall, BF16),
            pltpu.VMEM(tall, BF16),
        ],
        compiler_params=params(48),
    )(core, own_gram, oth_gram, own, oth)


def pick_kernel(c_ref, back_ref, out_ref):
    for i in range(6):
        out_ref[i] = back_ref[(i % 3) * 4 + 2 * (1 - c_ref[0]) + i // 3]


def pick(ctl, back):
    return pl.pallas_call(
        pick_kernel,
        in_specs=[SMEM, VMEM],
        out_specs=VMEM,
        out_shape=jax.ShapeDtypeStruct((6, SHARD, HALF), BF16),
        compiler_params=params(16),
    )(ctl, back)


def join_kernel(c_ref, own_ref, oth_ref, out_ref):
    c = c_ref[0]
    for i in range(6):
        slot = (i % 3) * 4 + 2 * c + i // 3
        own, oth = own_ref[slot], oth_ref[i]
        out_ref[i, :, :HALF] = jnp.where(c == 0, own, oth)
        out_ref[i, :, HALF:] = jnp.where(c == 0, oth, own)


def join(ctl, own, oth):
    return pl.pallas_call(
        join_kernel,
        in_specs=[SMEM, VMEM, VMEM],
        out_specs=VMEM,
        out_shape=jax.ShapeDtypeStruct((6, SHARD, FF), BF16),
        compiler_params=params(16),
    )(ctl, own, oth)


def swap(value):
    return lax.ppermute(value, "c", [(0, 1), (1, 0)])


def owner_rms(notes, owners):
    norms = jnp.sum(notes[:, 0].astype(F32) + notes[:, 16].astype(F32), axis=0)
    norms = norms.reshape(4, 128)[:, :12].reshape(owners.shape)
    me = (lax.axis_index("a") * 4 + lax.axis_index("b")) * 4 + lax.axis_index("y")
    return jnp.sqrt(jnp.sum(jnp.where(owners == me, norms, 0.0)) / (D * FF)).reshape(1)


def between(value, shift):
    pairs = []
    for a, b, y, x in itertools.product(range(4), repeat=4):
        if b != IDLE or y == shift:
            ends = ((a, b, y, x), ((a + shift) % 4, b, y, x))
            pairs.append(tuple(((h * 4 + i) * 4 + j) * 4 + k for h, i, j, k in ends))
    return lax.ppermute(value, ("a", "b", "y", "x"), pairs)


def gather(value):
    groups = [[(a * 4 + b) * 4 + x for a in range(4)] for b in range(IDLE) for x in range(4)]
    groups += [[(a * 4 + IDLE) * 4 + x for x in range(4)] for a in range(4)]
    return lax.all_gather(value, ("a", "b", "x"), axis=0, axis_index_groups=groups)


def shards(grad, momentum, owners):
    shape = grad.shape
    core, a, b = (lax.axis_index(name).astype(jnp.int32) for name in ("c", "a", "b"))
    y = lax.axis_index("y").astype(jnp.int32)
    ctl = jnp.stack([core, (b == IDLE).astype(jnp.int32), a, y])
    flat = (6, SHARD, FF)
    grad = pltpu.with_memory_space_constraint(grad.reshape(flat), pltpu.HBM)
    momentum = pltpu.with_memory_space_constraint(momentum.reshape(flat), pltpu.HBM)
    keep, send, sums = blend(ctl, grad, momentum)
    packed = pack(ctl, keep, swap(send), sums)
    own = lax.all_to_all(packed, ("b", "y"), 0, 0, tiled=True)
    oth = swap(own)
    partial = partial_gram(ctl, own, oth)
    parts = [partial[0]] + [between(partial[j], j) for j in (1, 2, 3)]
    momentum_new = new_momentum(grad, momentum, partial[0])
    *parts, momentum_new = lax.optimization_barrier((*parts, momentum_new))
    own_gram = gather(sum_parts(ctl, parts))
    oth_gram = swap(own_gram)
    finished = polynomial(ctl, own_gram, oth_gram, own, oth)
    back = lax.all_to_all(finished, ("b", "y"), 0, 0, tiled=True)
    update = join(ctl, back, swap(pick(ctl, back)))
    owned_rms = owner_rms(back[IDLE * 4 :], owners)
    return (momentum_new.reshape(shape), update.reshape(shape), owned_rms)


def solution(mesh):
    fine = Mesh(mesh.devices.reshape(4, 4, 4, 4, 2), ("a", "b", "y", "x", "c"))
    rows = ("a", "b", "y")
    wide = P(("x", "c"), None, rows, None)
    return jax.shard_map(
        shards, mesh=fine, in_specs=(wide, wide, P()), out_specs=(wide, wide, P(rows)), check_vma=False
    )
```
